256 devices in a mesh: tile: 16 (over y_lo, z), tf: 16 (over x, y_hi, core).
Axes of the slice: x: 4, y: 4 (y_hi: 2, y_lo: 2; y = y_hi * 2 + y_lo), z: 8, core: 2. Of those that a mesh axis runs over, the one named last changes fastest.
Arguments:
- test_field: float32 [16, 3, 16, 256, 1024], P('tf', None, None, 'tile'), may hold values from -6 to 6
- register: float32 [16, 3, 16, 256, 1024], P('tf', None, None, 'tile'), may hold values from -6 to 6
- velocity: bfloat16 [3, 16, 256, 1024], P(None, 'tf', 'tile'), may hold values from -6 to 6
- shear_shift: int32 [2], replicated, may hold values from 0 to 255
Outputs:
- new_field: float32 [16, 3, 16, 256, 1024], P('tf', None, None, 'tile')
- new_register: float32 [16, 3, 16, 256, 1024], P('tf', None, None, 'tile')
The draws below stay inside these ranges and needn't reach their ends.
Inputs may be any that keep to these rules, and one draw needn't show every extreme that they name: `shear_shift`: the two offsets are independent.
All inputs are finite; a program needn't handle non-finite values.
Results may differ from the reference program's by a relative error of at most 0.0065.
Values may be sent and summed in bfloat16 or wider, within the bound.
A program may use at most 128 MiB of HBM per device.

```python
import math
import jax
import jax.numpy as jnp
from jax import lax

NX = 1024
NZ = 16
TFIELDS = 16
NY = 256


def steps_of(rng, dims, split, least, largest):
    level = 1.0
    for position, shards_of in split:
        heights = jax.random.uniform(jax.random.fold_in(jax.random.fold_in(rng, 6), position), (shards_of,), jnp.float32, least / len(split), largest / len(split))
        level = level * jnp.repeat(jnp.exp(heights), dims[position] // shards_of).reshape((-1,) + (1,) * (len(dims) - 1 - position))
    return level


def centred(stream_key, extent, deviation, bound, split=(), dtype=jnp.bfloat16):
    drawn = deviation * jax.random.normal(stream_key, extent, jnp.float32)
    if split:
        drawn = drawn * steps_of(stream_key, extent, split, -0.22, 0.18)
    return jnp.clip(drawn, -bound, bound).astype(dtype)


def setup_inputs(seed: int = 0) -> dict:
    key_of = jax.random.split(jax.random.key(seed), 5)
    test_field = centred(key_of[0], (TFIELDS, 3, NZ, NY, NX), 1.0, 6.0, ((0, 16), (3, 16)), jnp.float32)
    register = centred(key_of[1], (TFIELDS, 3, NZ, NY, NX), 1.0, 6.0, ((0, 16), (3, 16)), jnp.float32)
    velocity = centred(key_of[2], (3, NZ, NY, NX), 1.0, 6.0, ((1, 16), (2, 16)))
    shear_shift = jax.random.randint(key_of[3], (2,), 0, NY).astype(jnp.int32)
    return dict(test_field=test_field, register=register, velocity=velocity, shear_shift=shear_shift)


DIFFUSIVITY = 0.1
TIME_STEP = 0.3
RK_ALPHA = -5.0 / 9.0
RK_BETA = 15.0 / 16.0
SWEEP_SPEED = 0.75
STRETCH_RATE = 0.375


def first_derivative(shifted):
    return (45.0 * (shifted(1) - shifted(-1)) - 9.0 * (shifted(2) - shifted(-2)) + (shifted(3) - shifted(-3))) / 60.0


def second_derivative(shifted):
    return (-49.0 / 18.0) * shifted(0) + 1.5 * (shifted(1) + shifted(-1)) - 0.15 * (shifted(2) + shifted(-2)) + (shifted(3) + shifted(-3)) / 90.0


def test_pattern(field_index, planes):
    height = jnp.arange(planes).astype(jnp.float32)
    wavenumber = (field_index // 4 + 1).astype(jnp.float32)
    phase = 2.0 * math.pi * wavenumber[:, None] * height[None, :] / planes
    profile = jnp.where(((field_index // 2) % 2 == 0)[:, None], jnp.cos(phase), jnp.sin(phase))
    component = field_index % 2
    selector = (jnp.arange(3)[None, :] == component[:, None]).astype(jnp.float32)
    return (selector[:, :, None] * profile[:, None, :])[:, :, :, None, None]


def cross_emf(velocity, summed):
    vel = velocity.astype(jnp.float32)
    fld = summed.astype(jnp.float32)
    emf_x = vel[1] * fld[:, 2] - vel[2] * fld[:, 1]
    emf_y = vel[2] * fld[:, 0] - vel[0] * fld[:, 2]
    emf_z = vel[0] * fld[:, 1] - vel[1] * fld[:, 0]
    return jnp.stack([emf_x, emf_y, emf_z], 1).astype(jnp.bfloat16)


def tendency(field, view, width):
    def deriv(name, axis, channel):
        def shifted(offset):
            return view(name, axis, offset, channel)
        return first_derivative(shifted)

    def second(axis):
        def shifted(offset):
            return view("field", axis, offset, slice(None))
        return second_derivative(shifted)

    curl_x = deriv("emf", 1, 2) - deriv("emf", 2, 1)
    curl_y = deriv("emf", 2, 0) - deriv("emf", 0, 2)
    curl_z = deriv("emf", 0, 1) - deriv("emf", 1, 0)
    curl = jnp.stack([curl_x, curl_y, curl_z], 1)
    laplace = second(0) + second(1) + second(2)
    field_dy = deriv("field", 1, slice(None))
    xpos = jnp.arange(width).astype(jnp.float32)
    sweep = -SWEEP_SPEED * (2.0 * xpos / (width - 1) - 1.0)
    rate = curl + DIFFUSIVITY * laplace - sweep * field_dy
    return rate.at[:, 1].add(-STRETCH_RATE * field[:, 0])


def shear_pad(array, shear_shift):
    lower = jnp.roll(array[..., NX - 3:], -shear_shift[0], axis=-2)
    upper = jnp.roll(array[..., :3], -shear_shift[1], axis=-2)
    return jnp.concatenate([lower, array, upper], axis=-1)


def reference(test_field, register, velocity, shear_shift):
    def one_field(field_index):
        field = lax.dynamic_index_in_dim(test_field, field_index, 0, keepdims=True)
        store = lax.dynamic_index_in_dim(register, field_index, 0, keepdims=True)
        pattern = test_pattern(field_index[None], NZ)
        summed = (field + pattern).astype(jnp.bfloat16)
        emf = cross_emf(velocity, summed)
        arrays = {"field": field, "emf": emf}
        padded = {"field": shear_pad(field, shear_shift), "emf": shear_pad(emf, shear_shift)}

        def view(name, axis, offset, channel):
            if axis == 0:
                return padded[name][:, channel][..., 3 + offset:3 + offset + NX].astype(jnp.float32)
            base = arrays[name][:, channel]
            if axis == 1:
                return jnp.roll(base, -offset, axis=-2).astype(jnp.float32)
            return jnp.roll(base, -offset, axis=-3).astype(jnp.float32)

        rate = tendency(field, view, NX)
        next_register = RK_ALPHA * store + TIME_STEP * rate
        next_field = field + RK_BETA * next_register
        return next_field[0], next_register[0]

    indices = jnp.arange(TFIELDS).astype(jnp.int32)
    new_field, new_register = lax.map(one_field, indices)
    return (new_field, new_register)
```

```python
import functools
import math

import jax
import jax.numpy as jnp
import ml_dtypes
import numpy as np
from jax import lax
from jax.experimental import pallas as pl
from jax.experimental.pallas import tpu as pltpu
from jax.sharding import PartitionSpec as P

BF = jnp.bfloat16
F32 = jnp.float32
TIME_STEP = 0.3
RK_ALPHA = -5.0 / 9.0
RK_BETA = 15.0 / 16.0
SWEEP_SPEED = 0.75
STRETCH_RATE = 0.375
SCALE = TIME_STEP / 60.0

FIRST = {-3: -1, -2: 9, -1: -45, 1: 45, 2: -9, 3: 1}
SECOND = {-3: 2, -2: -27, -1: 270, 0: -490, 1: 270, 2: -27, 3: 2}

NZ, ROWS, NX = 16, 16, 1024
CELLS = NZ * ROWS
BLOCK = 256
BLOCKS = NX // BLOCK
ORDER = (0, 3, 1, 2)
HALO = 3 * NZ


def band(coefs):
    out = np.zeros((BLOCK, BLOCK))
    for offset, value in coefs.items():
        for x in range(BLOCK):
            if 0 <= x + offset < BLOCK:
                out[x + offset, x] = value
    return out


def band_edges(coefs):
    out = np.zeros((256, BLOCK))
    for offset, value in coefs.items():
        for x in range(BLOCK):
            if x + offset < 0:
                out[128 + x + offset, x] = value
            elif x + offset >= BLOCK:
                out[128 + x + offset - BLOCK, x] = value
    return out


def rows_y(coefs):
    out = np.zeros((CELLS, CELLS))
    for offset, value in coefs.items():
        for y in range(ROWS):
            if 0 <= y + offset < ROWS:
                for z in range(NZ):
                    out[z * ROWS + y, z * ROWS + y + offset] += value
    return out


def rows_z(coefs):
    out = np.zeros((CELLS, CELLS))
    for offset, value in coefs.items():
        for z in range(NZ):
            for y in range(ROWS):
                out[z * ROWS + y, (z + offset) % NZ * ROWS + y] += value
    return out


def rows_out(coefs):
    out = np.zeros((2, 3, NZ, CELLS))
    for z in range(NZ):
        for j in range(3):
            for s in range(3):
                low, high = s - 3 - j, 3 + s - j
                if low in coefs and low >= -3:
                    out[0, j, z, z * ROWS + ROWS - 3 + s] = coefs[low]
                if high <= 3:
                    out[1, j, z, z * ROWS + s] = coefs[high]
    return out.reshape(2 * HALO, CELLS)


def strip_out(coefs):
    out = np.zeros((256, 128))
    for group in range(16):
        for cell in range(3):
            for s in range(3):
                low, high = s - 3 - cell, 3 + s - cell
                if low >= -3:
                    out[253 + s, group * 8 + cell] = coefs[low]
                if high <= 3:
                    out[s, group * 8 + 4 + cell] = coefs[high]
    return out


def halo_in():
    out = np.zeros((CELLS, 2, 3, NZ))
    for z in range(NZ):
        for j in range(3):
            out[z * ROWS + j, 0, j, z] = 1
            out[z * ROWS + ROWS - 3 + j, 1, j, z] = 1
    return out.reshape(CELLS, 2 * HALO)


def strip_in():
    out = np.zeros((BLOCKS, 128, BLOCK))
    for lane in range(128):
        cell = lane % 4
        if cell < 3:
            if lane % 8 < 4:
                out[0, lane, cell] = 1
            else:
                out[BLOCKS - 1, lane, BLOCK - 3 + cell] = 1
    return out


def small(array):
    return jnp.asarray(np.asarray(array).astype(ml_dtypes.bfloat16))


def profiles():
    z = np.arange(NZ, dtype=np.float32)
    out = np.zeros((16, 2, NZ), np.float32)
    for k in range(16):
        phase = np.float32(2.0 * math.pi) * np.float32(k // 4 + 1) * z / np.float32(NZ)
        out[k, k % 2] = np.cos(phase) if k // 2 % 2 == 0 else np.sin(phase)
    return out.reshape(-1)


def dot(a, b):
    return jnp.dot(a, b, preferred_element_type=F32)


def exchange(
    tiles, profile, field_hbm, register_hbm, velocity_hbm, zy_hbm, out_hbm, x_hbm, edge_hbm, strip_hbm,
    base, halo, strips,
    field, register, vel, work, sums, zy, outw, xw, edgew, stripw,
    load_sem, const_sem, vsend, vrecv, hsend, hrecv, ssend, srecv,
):
    t = lax.axis_index("tile")
    k = lax.axis_index("tf")
    xi, hc = k // 4, k % 4
    core = k % 2
    plus, minus = (xi + 1) % 4, (xi + 3) % 4
    opposite = (xi + 2) % 4
    other = hc + 2 - (hc // 2) * 4
    at_plus, at_minus = plus * 4 + hc, minus * 4 + hc
    partner = xi * 4 + other
    sibling = k + 1 - 2 * core

    own_velocity = pltpu.make_async_copy(velocity_hbm.at[:, 0], vel.at[k], load_sem.at[0])
    own_velocity.start()
    load_field = pltpu.make_async_copy(field_hbm, field, load_sem.at[1])
    load_field.start()
    pairs = ((zy_hbm, zy), (out_hbm, outw), (x_hbm, xw), (edge_hbm, edgew), (strip_hbm, stripw))
    consts = [pltpu.make_async_copy(a, b, const_sem.at[i]) for i, (a, b) in enumerate(pairs)]
    for copy in consts:
        copy.start()
    load_register = pltpu.make_async_copy(register_hbm, register, load_sem.at[2])
    load_register.start()

    barrier = pltpu.get_barrier_semaphore()
    for peer in (at_plus, at_minus, partner, sibling):
        pl.semaphore_signal(barrier, inc=1, device_id={"tf": peer})
    for step in range(1, tiles):
        pl.semaphore_signal(barrier, inc=1, device_id={"tile": (t + step) % tiles})
    pl.semaphore_wait(barrier, 4 + tiles - 1)

    started = []

    def lanes(part):
        return pl.ds(ORDER[part] * BLOCK, BLOCK)

    def plane_copy(plane, part, kind, peer):
        block = vel.at[plane, :, :, lanes(part)]
        return pltpu.make_async_remote_copy(
            src_ref=block,
            dst_ref=block,
            send_sem=vsend.at[part, kind],
            recv_sem=vrecv.at[part, plane],
            device_id={"tf": peer},
        )

    def send(plane, part, kind, peer):
        copy = plane_copy(plane, part, kind, peer)
        copy.start()
        started.append(copy)

    def arrived(plane, part):
        plane_copy(plane, part, 0, sibling).wait_recv()

    def of(x, h):
        return x * 4 + h

    own_velocity.wait()
    for part in range(BLOCKS):
        send(k, part, 0, partner)
        send(k, part, 1, at_plus)
        send(k, part, 2, at_minus)
        send(k, part, 3, sibling)
    for part in range(BLOCKS):
        arrived(partner, part)
        send(partner, part, 4, at_plus)
        send(partner, part, 5, at_minus)
        send(partner, part, 6, sibling)

    def forward(part):
        arrived(of(minus, hc), part)
        send(of(minus, hc), part, 7, at_plus)
        send(of(minus, hc), part, 8, sibling)
        arrived(of(plus, hc), part)
        send(of(plus, hc), part, 9, sibling)
        arrived(of(plus, other), part)
        send(of(plus, other), part, 10, at_minus)
        send(of(plus, other), part, 11, sibling)
        arrived(of(minus, other), part)
        send(of(minus, other), part, 12, sibling)

    def last_forward(part):
        arrived(of(opposite, hc), part)
        send(of(opposite, hc), part, 13, sibling)
        arrived(of(opposite, other), part)
        send(of(opposite, other), part, 14, sibling)

    def from_sibling(part):
        flip = 1 - 2 * core
        for x in range(4):
            for h in range(2):
                arrived(x * 4 + h * 2 + core + flip, part)

    def emf_of(part):
        block = lanes(part)
        xpos = (lax.broadcasted_iota(jnp.int32, (ROWS, BLOCK), 1) + ORDER[part] * BLOCK).astype(F32)
        sweep = -SWEEP_SPEED * (2.0 * xpos / (NX - 1) - 1.0)

        def plane(z, carry):
            rows = pl.ds(pl.multiple_of(z * ROWS, ROWS), ROWS)
            f = [field[c, rows, block] for c in range(3)]
            v = [vel[z, c, :, block].astype(F32) for c in range(3)]
            summed = [
                (f[0] + profile[k * 32 + z]).astype(BF).astype(F32),
                (f[1] + profile[k * 32 + 16 + z]).astype(BF).astype(F32),
                f[2].astype(BF).astype(F32),
            ]
            emf_x = v[1] * summed[2] - v[2] * summed[1]
            emf_y = v[2] * summed[0] - v[0] * summed[2]
            emf_z = v[0] * summed[1] - v[1] * summed[0]
            mixed = (emf_z - sweep * f[0], -(sweep * f[1]), -emf_x - sweep * f[2])
            for c, value in enumerate((-emf_y, emf_x, emf_z)):
                work[c, rows, block] = value.astype(BF)
            for c in range(3):
                work[c, pl.ds(pl.multiple_of(CELLS + z * ROWS, ROWS), ROWS), block] = mixed[c].astype(BF)
                work[c, pl.ds(pl.multiple_of(2 * CELLS + z * ROWS, ROWS), ROWS), block] = (f[c] * (1.0 / 30.0)).astype(BF)
            return carry

        lax.fori_loop(0, NZ, plane, 0)

    def halo_copies(part):
        block = lanes(part)
        out = []
        for side, peer in ((0, (t + 1) % tiles), (1, (t + tiles - 1) % tiles)):
            out.append(
                pltpu.make_async_remote_copy(
                    src_ref=sums.at[:, side, :, block],
                    dst_ref=halo.at[:, side, :, block],
                    send_sem=hsend.at[side, part],
                    recv_sem=hrecv.at[side, part],
                    device_id={"tile": peer},
                )
            )
        return out

    def halo_of(part):
        block = lanes(part)
        for c in range(3):
            total = dot(outw[...], work[c, CELLS:, block]).astype(BF)
            for side in range(2):
                sums[c, side, :, block] = total[side * HALO : (side + 1) * HALO]
        for copy in halo_copies(part):
            copy.start()
            started.append(copy)

    def strip_copy(step, at):
        return pltpu.make_async_remote_copy(
            src_ref=strips.at[:, pl.ds(pl.multiple_of(at * ROWS, ROWS), ROWS), :],
            dst_ref=strips.at[:, pl.ds(pl.multiple_of(at * ROWS, ROWS), ROWS), :],
            send_sem=ssend.at[step],
            recv_sem=srecv.at[at],
            device_id={"tile": (t + step) % tiles},
        )

    def strips_of():
        row = lax.broadcasted_iota(jnp.int32, (CELLS, 128), 0)
        lane = lax.broadcasted_iota(jnp.int32, (CELLS, 128), 1)
        own = (row // ROWS) == (lane // 8)

        def ends(c, part):
            rows = slice(part * CELLS, (part + 1) * CELLS)
            return jnp.concatenate([work[c, rows, :128], work[c, rows, NX - 128 :]], axis=1)

        for c in range(3):
            total = dot(ends(c, 2), stripw[:256])
            if c == 1:
                total += dot(ends(2, 0), stripw[256:])
            if c == 2:
                total += dot(ends(0, 0), stripw[256:])
            packed = jnp.sum(jnp.where(own, total, 0.0).reshape(NZ, ROWS, 128), axis=0)
            strips[c, pl.ds(pl.multiple_of(t * ROWS, ROWS), ROWS), :] = packed.astype(BF)
        for step in range(1, tiles):
            copy = strip_copy(step, t)
            copy.start()
            started.append(copy)

    forward(0)
    load_field.wait()
    for copy in consts:
        copy.wait()
    for part in range(BLOCKS):
        last_forward(part)
        if part + 1 < BLOCKS:
            forward(part + 1)
        from_sibling(part)
        emf_of(part)
        halo_of(part)
        if part == 1:
            strips_of()

    load_register.wait()
    for b in range(BLOCKS):
        block = slice(b * BLOCK, (b + 1) * BLOCK)

        def ends(c, part):
            rows = slice(part * CELLS, (part + 1) * CELLS)
            before = work[c, rows, b * BLOCK - 128 : b * BLOCK] if b > 0 else None
            after = work[c, rows, (b + 1) * BLOCK : (b + 1) * BLOCK + 128] if b + 1 < BLOCKS else None
            if before is None:
                return after, slice(128, 256)
            if after is None:
                return before, slice(0, 128)
            return jnp.concatenate([before, after], axis=1), slice(0, 256)

        for c in range(3):
            if c < 2:
                total = dot(zy[...], work[c, :, block])
            else:
                total = dot(zy[:, CELLS:], work[c, CELLS:, block])
            total += dot(work[c, 2 * CELLS :, block], xw[:256])
            far, near = ends(c, 2)
            total += dot(far, edgew[:256][near])
            if c > 0:
                source = 2 if c == 1 else 0
                total += dot(work[source, :CELLS, block], xw[256:])
                far, near = ends(source, 0)
                total += dot(far, edgew[256:][near])
            result = RK_ALPHA * register[c, :, block] + SCALE * total
            if c == 1:
                result -= TIME_STEP * STRETCH_RATE * field[0, :, block]
            base[c, :, block] = result

    for part in range(BLOCKS):
        for copy in halo_copies(part):
            copy.wait_recv()
    for step in range(1, tiles):
        strip_copy(step, (t + step) % tiles).wait_recv()
    for copy in started:
        copy.wait_send()


def finish(shift, field, base, halo, strips, spread, ends, new_field, new_register, ghost):
    @pl.when(pl.program_id(0) == 0)
    def _():
        t = lax.axis_index("tile")
        total = strips.shape[1]
        place = lax.broadcasted_iota(jnp.int32, (ROWS, total), 0) + t * ROWS
        source = lax.broadcasted_iota(jnp.int32, (ROWS, total), 1)
        lane = lax.broadcasted_iota(jnp.int32, (ROWS, 128), 1)
        picks = [jnp.where((place + shift[side]) % total == source, 1.0, 0.0).astype(BF) for side in range(2)]
        for c in range(3):
            low, high = (dot(pick, strips[c]) for pick in picks)
            both = jnp.where(lane % 8 < 4, low, high)
            for z in range(NZ):
                ghost[c, z * ROWS : (z + 1) * ROWS] = jnp.where(lane // 8 == z, both, 0.0).astype(BF)

    for c in range(3):
        total = dot(spread[...], halo[c].reshape(2 * HALO, BLOCK)) + dot(ghost[c], ends[0])
        register = base[c] + SCALE * total
        new_register[c] = register
        new_field[c] = field[c] + RK_BETA * register


def body(tiles, test_field, register, velocity, shear_shift):
    field = test_field.reshape(3, CELLS, NX)
    reg = register.reshape(3, CELLS, NX)
    zy = small(np.concatenate([rows_z(FIRST), rows_y(FIRST), rows_y(SECOND) + rows_z(SECOND)], 1))
    outw = small(np.concatenate([rows_out(FIRST), rows_out(SECOND)], 1))
    xw = small(np.concatenate([band(SECOND), -band(FIRST)], 0))
    edgew = small(np.concatenate([band_edges(SECOND), -band_edges(FIRST)], 0))
    stripw = small(np.concatenate([strip_out(SECOND), -strip_out(FIRST)], 0))
    anywhere = pl.BlockSpec(memory_space=pl.ANY)
    vmem = pl.BlockSpec(memory_space=pltpu.VMEM)
    dma = pltpu.SemaphoreType.DMA
    base, halo, strips = pl.pallas_call(
        functools.partial(exchange, tiles),
        out_shape=(
            jax.ShapeDtypeStruct((3, CELLS, NX), F32),
            jax.ShapeDtypeStruct((3, 2, HALO, NX), BF),
            jax.ShapeDtypeStruct((3, tiles * ROWS, 128), BF),
        ),
        in_specs=[pl.BlockSpec(memory_space=pltpu.SMEM)] + [anywhere] * 8,
        out_specs=(vmem, vmem, vmem),
        scratch_shapes=[
            pltpu.VMEM((3, CELLS, NX), F32),
            pltpu.VMEM((3, CELLS, NX), F32),
            pltpu.VMEM((16, 3, ROWS, NX), BF),
            pltpu.VMEM((3, 3 * CELLS, NX), BF),
            pltpu.VMEM((3, 2, HALO, NX), BF),
            pltpu.VMEM(zy.shape, BF),
            pltpu.VMEM(outw.shape, BF),
            pltpu.VMEM(xw.shape, BF),
            pltpu.VMEM(edgew.shape, BF),
            pltpu.VMEM(stripw.shape, BF),
            dma((3,)),
            dma((5,)),
            dma((BLOCKS, 15)),
            dma((BLOCKS, 16)),
            dma((2, BLOCKS)),
            dma((2, BLOCKS)),
            dma((tiles,)),
            dma((tiles,)),
        ],
        compiler_params=pltpu.CompilerParams(
            collective_id=0, has_side_effects=True, vmem_limit_bytes=40 * 2**20
        ),
        name="exchange",
    )(jnp.asarray(profiles()), field, reg, velocity, zy, outw, xw, edgew, stripw)

    spread, ends = small(halo_in()), small(strip_in())
    whole = pl.BlockSpec((3, CELLS, BLOCK), lambda b: (0, 0, b))
    new_field, new_register = pl.pallas_call(
        finish,
        grid=(BLOCKS,),
        out_shape=(jax.ShapeDtypeStruct((3, CELLS, NX), F32),) * 2,
        in_specs=[
            pl.BlockSpec(memory_space=pltpu.SMEM),
            whole,
            whole,
            pl.BlockSpec((3, 2, HALO, BLOCK), lambda b: (0, 0, 0, b)),
            pl.BlockSpec((3, tiles * ROWS, 128), lambda b: (0, 0, 0)),
            pl.BlockSpec((CELLS, 2 * HALO), lambda b: (0, 0)),
            pl.BlockSpec((1, 128, BLOCK), lambda b: (b, 0, 0)),
        ],
        out_specs=(whole, whole),
        scratch_shapes=[pltpu.VMEM((3, CELLS, 128), BF)],
        compiler_params=pltpu.CompilerParams(vmem_limit_bytes=24 * 2**20),
        name="finish",
    )(shear_shift, field, base, halo, strips, spread, ends)
    return new_field.reshape(test_field.shape), new_register.reshape(register.shape)


def solution(mesh):
    cells = P("tf", None, None, "tile", None)
    return jax.shard_map(
        functools.partial(body, mesh.shape["tile"]),
        mesh=mesh,
        in_specs=(cells, cells, P(None, "tf", "tile", None), P()),
        out_specs=(cells, cells),
        check_vma=False,
    )
```

```python
import functools
import math

import jax
import jax.numpy as jnp
import ml_dtypes
import numpy as np
from jax import lax
from jax.experimental import pallas as pl
from jax.experimental.pallas import tpu as pltpu
from jax.sharding import PartitionSpec as P

BF = jnp.bfloat16
F32 = jnp.float32
TIME_STEP = 0.3
RK_ALPHA = -5.0 / 9.0
RK_BETA = 15.0 / 16.0
SWEEP_SPEED = 0.75
STRETCH_RATE = 0.375
SCALE = TIME_STEP / 60.0

FIRST = {-3: -1, -2: 9, -1: -45, 1: 45, 2: -9, 3: 1}
SECOND = {-3: 2, -2: -27, -1: 270, 0: -490, 1: 270, 2: -27, 3: 2}

NZ, ROWS, NX = 16, 16, 1024
CELLS = NZ * ROWS
BLOCK = 256
BLOCKS = NX // BLOCK
PARTS = ((0, 3), (1, 2))
ORDER = (0, 3, 1, 2)
HALO = 3 * NZ
WIDTH = 2 * BLOCK


def band(coefs):
    out = np.zeros((BLOCK, BLOCK))
    for offset, value in coefs.items():
        for x in range(BLOCK):
            if 0 <= x + offset < BLOCK:
                out[x + offset, x] = value
    return out


def band_edges(coefs):
    out = np.zeros((256, BLOCK))
    for offset, value in coefs.items():
        for x in range(BLOCK):
            if x + offset < 0:
                out[128 + x + offset, x] = value
            elif x + offset >= BLOCK:
                out[128 + x + offset - BLOCK, x] = value
    return out


def rows_y(coefs):
    out = np.zeros((CELLS, CELLS))
    for offset, value in coefs.items():
        for y in range(ROWS):
            if 0 <= y + offset < ROWS:
                for z in range(NZ):
                    out[z * ROWS + y, z * ROWS + y + offset] += value
    return out


def rows_z(coefs):
    out = np.zeros((CELLS, CELLS))
    for offset, value in coefs.items():
        for z in range(NZ):
            for y in range(ROWS):
                out[z * ROWS + y, (z + offset) % NZ * ROWS + y] += value
    return out


def rows_out(coefs):
    out = np.zeros((2, 3, NZ, CELLS))
    for z in range(NZ):
        for j in range(3):
            for s in range(3):
                low, high = s - 3 - j, 3 + s - j
                if low in coefs and low >= -3:
                    out[0, j, z, z * ROWS + ROWS - 3 + s] = coefs[low]
                if high <= 3:
                    out[1, j, z, z * ROWS + s] = coefs[high]
    return out.reshape(2 * HALO, CELLS)


def strip_out(coefs):
    out = np.zeros((256, 128))
    for group in range(16):
        for cell in range(3):
            for s in range(3):
                low, high = s - 3 - cell, 3 + s - cell
                if low >= -3:
                    out[253 + s, group * 8 + cell] = coefs[low]
                if high <= 3:
                    out[s, group * 8 + 4 + cell] = coefs[high]
    return out


def halo_in():
    out = np.zeros((CELLS, 2, 3, NZ))
    for z in range(NZ):
        for j in range(3):
            out[z * ROWS + j, 0, j, z] = 1
            out[z * ROWS + ROWS - 3 + j, 1, j, z] = 1
    return out.reshape(CELLS, 2 * HALO)


def strip_in():
    out = np.zeros((2, 128, BLOCK))
    for lane in range(128):
        cell = lane % 4
        if cell < 3:
            if lane % 8 < 4:
                out[0, lane, cell] = 1
            else:
                out[1, lane, BLOCK - 3 + cell] = 1
    return out


def small(array):
    return jnp.asarray(np.asarray(array).astype(ml_dtypes.bfloat16))


def profiles():
    z = np.arange(NZ, dtype=np.float32)
    out = np.zeros((16, 2, NZ), np.float32)
    for k in range(16):
        phase = np.float32(2.0 * math.pi) * np.float32(k // 4 + 1) * z / np.float32(NZ)
        out[k, k % 2] = np.cos(phase) if k // 2 % 2 == 0 else np.sin(phase)
    return out.reshape(-1)


def dot(a, b):
    return jnp.dot(a, b, preferred_element_type=F32)


def exchange(
    tiles, profile, field_hbm, register_hbm, velocity_hbm, zy_hbm, out_hbm, x_hbm, edge_hbm, strip_hbm,
    base, field, halo, strips,
    register, vel, work, sums, zy, outw, xw, edgew, stripw,
    load_sem, const_sem, vsend, vrecv, hsend, hrecv, ssend, srecv,
):
    t = lax.axis_index("tile")
    k = lax.axis_index("tf")
    xi, hc = k // 4, k % 4
    core = k % 2
    plus, minus = (xi + 1) % 4, (xi + 3) % 4
    opposite = (xi + 2) % 4
    other = hc + 2 - (hc // 2) * 4
    at_plus, at_minus, at_opposite = plus * 4 + hc, minus * 4 + hc, opposite * 4 + hc
    partner = xi * 4 + other
    sibling = k + 1 - 2 * core

    own_velocity = []
    for i, (low, high, to) in enumerate(((0, 1, 0), (3, 4, 1), (1, 3, 2))):
        source = velocity_hbm.at[:, 0, :, pl.ds(low * BLOCK, (high - low) * BLOCK)]
        target = vel.at[k, :, :, pl.ds(to * BLOCK, (high - low) * BLOCK)]
        own_velocity.append(pltpu.make_async_copy(source, target, load_sem.at[i]))
    load_field = pltpu.make_async_copy(field_hbm, field, load_sem.at[3])
    load_register = pltpu.make_async_copy(register_hbm, register, load_sem.at[4])
    pairs = ((zy_hbm, zy), (out_hbm, outw), (x_hbm, xw), (edge_hbm, edgew), (strip_hbm, stripw))
    consts = [pltpu.make_async_copy(a, b, const_sem.at[i]) for i, (a, b) in enumerate(pairs)]
    for copy in (*own_velocity, load_field, *consts, load_register):
        copy.start()

    barrier = pltpu.get_barrier_semaphore()
    for peer in (at_plus, at_minus, at_opposite, partner, sibling):
        pl.semaphore_signal(barrier, inc=1, device_id={"tf": peer})
    for step in range(1, tiles):
        pl.semaphore_signal(barrier, inc=1, device_id={"tile": (t + step) % tiles})
    pl.semaphore_wait(barrier, 5 + tiles - 1)

    started = []

    def plane_copy(plane, part, kind, peer):
        block = vel.at[plane, :, :, pl.ds(part * WIDTH, WIDTH)]
        return pltpu.make_async_remote_copy(
            src_ref=block,
            dst_ref=block,
            send_sem=vsend.at[part, kind],
            recv_sem=vrecv.at[part, plane],
            device_id={"tf": peer},
        )

    def send(plane, part, kind, peer):
        copy = plane_copy(plane, part, kind, peer)
        copy.start()
        started.append(copy)

    def arrived(plane, part):
        plane_copy(plane, part, 0, sibling).wait_recv()

    def send_own(part):
        for kind, peer in enumerate((partner, at_opposite, at_plus, at_minus, sibling)):
            send(k, part, kind, peer)

    def relay(part):
        arrived(partner, part)
        send(partner, part, 5, at_plus)
        send(partner, part, 6, at_minus)
        send(partner, part, 7, sibling)
        arrived(at_opposite, part)
        send(at_opposite, part, 8, partner)
        send(at_opposite, part, 9, sibling)
        arrived(at_plus, part)
        send(at_plus, part, 10, sibling)
        arrived(at_minus, part)
        send(at_minus, part, 11, sibling)

    def last_relay(part):
        for i, x in enumerate((plus, minus, opposite)):
            arrived(x * 4 + other, part)
            send(x * 4 + other, part, 12 + i, sibling)

    def from_sibling(part):
        for x in range(4):
            for h in range(2):
                arrived(x * 4 + h * 2 + 1 - core, part)

    def emf_of(b):
        block = pl.ds(b * BLOCK, BLOCK)
        stored = pl.ds(ORDER.index(b) * BLOCK, BLOCK)
        xpos = (lax.broadcasted_iota(jnp.int32, (ROWS, BLOCK), 1) + b * BLOCK).astype(F32)
        sweep = -SWEEP_SPEED * (2.0 * xpos / (NX - 1) - 1.0)

        def plane(z, carry):
            rows = pl.ds(pl.multiple_of(z * ROWS, ROWS), ROWS)
            f = [field[c, rows, block] for c in range(3)]
            v = [vel[z, c, :, stored].astype(F32) for c in range(3)]
            summed = [
                (f[0] + profile[k * 32 + z]).astype(BF).astype(F32),
                (f[1] + profile[k * 32 + 16 + z]).astype(BF).astype(F32),
                f[2].astype(BF).astype(F32),
            ]
            emf_x = v[1] * summed[2] - v[2] * summed[1]
            emf_y = v[2] * summed[0] - v[0] * summed[2]
            emf_z = v[0] * summed[1] - v[1] * summed[0]
            mixed = (emf_z - sweep * f[0], -(sweep * f[1]), -emf_x - sweep * f[2])
            for c, value in enumerate((-emf_y, emf_x, emf_z)):
                work[c, rows, block] = value.astype(BF)
            for c in range(3):
                work[c, pl.ds(pl.multiple_of(CELLS + z * ROWS, ROWS), ROWS), block] = mixed[c].astype(BF)
                work[c, pl.ds(pl.multiple_of(2 * CELLS + z * ROWS, ROWS), ROWS), block] = (f[c] * (1.0 / 30.0)).astype(BF)
            return carry

        lax.fori_loop(0, NZ, plane, 0)

    def halo_copies(b):
        block = pl.ds(b * BLOCK, BLOCK)
        out = []
        for side, peer in ((0, (t + 1) % tiles), (1, (t + tiles - 1) % tiles)):
            out.append(
                pltpu.make_async_remote_copy(
                    src_ref=sums.at[:, side, :, block],
                    dst_ref=halo.at[:, side, :, block],
                    send_sem=hsend.at[side, b],
                    recv_sem=hrecv.at[side, b],
                    device_id={"tile": peer},
                )
            )
        return out

    def halo_of(b):
        block = pl.ds(b * BLOCK, BLOCK)
        for c in range(3):
            total = dot(outw[...], work[c, CELLS:, block]).astype(BF)
            for side in range(2):
                sums[c, side, :, block] = total[side * HALO : (side + 1) * HALO]
        for copy in halo_copies(b):
            copy.start()
            started.append(copy)

    def strip_copy(step, at):
        return pltpu.make_async_remote_copy(
            src_ref=strips.at[:, pl.ds(pl.multiple_of(at * ROWS, ROWS), ROWS), :],
            dst_ref=strips.at[:, pl.ds(pl.multiple_of(at * ROWS, ROWS), ROWS), :],
            send_sem=ssend.at[step],
            recv_sem=srecv.at[at],
            device_id={"tile": (t + step) % tiles},
        )

    def strips_of():
        row = lax.broadcasted_iota(jnp.int32, (CELLS, 128), 0)
        lane = lax.broadcasted_iota(jnp.int32, (CELLS, 128), 1)
        own = (row // ROWS) == (lane // 8)

        def ends(c, part):
            rows = slice(part * CELLS, (part + 1) * CELLS)
            return jnp.concatenate([work[c, rows, :128], work[c, rows, NX - 128 :]], axis=1)

        for c in range(3):
            total = dot(ends(c, 2), stripw[:256])
            if c == 1:
                total += dot(ends(2, 0), stripw[256:])
            if c == 2:
                total += dot(ends(0, 0), stripw[256:])
            packed = jnp.sum(jnp.where(own, total, 0.0).reshape(NZ, ROWS, 128), axis=0)
            strips[c, pl.ds(pl.multiple_of(t * ROWS, ROWS), ROWS), :] = packed.astype(BF)
        for step in range(1, tiles):
            copy = strip_copy(step, t)
            copy.start()
            started.append(copy)

    for copy in own_velocity:
        copy.wait()
    for part in range(2):
        send_own(part)
    for part in range(2):
        relay(part)
    load_field.wait()
    for copy in consts:
        copy.wait()
    for part in range(2):
        last_relay(part)
        from_sibling(part)
        for b in PARTS[part]:
            emf_of(b)
        if part == 0:
            strips_of()
        for b in PARTS[part]:
            halo_of(b)

    load_register.wait()
    for b in range(BLOCKS):
        block = slice(b * BLOCK, (b + 1) * BLOCK)

        def ends(c, part):
            rows = slice(part * CELLS, (part + 1) * CELLS)
            before = work[c, rows, b * BLOCK - 128 : b * BLOCK] if b > 0 else None
            after = work[c, rows, (b + 1) * BLOCK : (b + 1) * BLOCK + 128] if b + 1 < BLOCKS else None
            if before is None:
                return after, slice(128, 256)
            if after is None:
                return before, slice(0, 128)
            return jnp.concatenate([before, after], axis=1), slice(0, 256)

        for c in range(3):
            if c < 2:
                total = dot(zy[...], work[c, :, block])
            else:
                total = dot(zy[:, CELLS:], work[c, CELLS:, block])
            total += dot(work[c, 2 * CELLS :, block], xw[:256])
            far, near = ends(c, 2)
            total += dot(far, edgew[:256][near])
            if c > 0:
                source = 2 if c == 1 else 0
                total += dot(work[source, :CELLS, block], xw[256:])
                far, near = ends(source, 0)
                total += dot(far, edgew[256:][near])
            result = RK_ALPHA * register[c, :, block] + SCALE * total
            if c == 1:
                result -= TIME_STEP * STRETCH_RATE * field[0, :, block]
            base[c, :, block] = result

    for b in range(BLOCKS):
        for copy in halo_copies(b):
            copy.wait_recv()
    for step in range(1, tiles):
        strip_copy(step, (t + step) % tiles).wait_recv()
    for copy in started:
        copy.wait_send()


def finish(shift, base, field, halo, strips, spread, ends, field_out, register_out, ghost, new_field, new_register, sem):
    t = lax.axis_index("tile")
    total = strips.shape[1]
    place = lax.broadcasted_iota(jnp.int32, (ROWS, total), 0) + t * ROWS
    source = lax.broadcasted_iota(jnp.int32, (ROWS, total), 1)
    lane = lax.broadcasted_iota(jnp.int32, (ROWS, 128), 1)
    picks = [jnp.where((place + shift[side]) % total == source, 1.0, 0.0).astype(BF) for side in range(2)]
    for c in range(3):
        low, high = (dot(pick, strips[c]) for pick in picks)
        both = jnp.where(lane % 8 < 4, low, high)
        for z in range(NZ):
            ghost[c, z * ROWS : (z + 1) * ROWS] = jnp.where(lane // 8 == z, both, 0.0).astype(BF)

    copies = []
    for c in range(3):
        for b in range(BLOCKS):
            block = slice(b * BLOCK, (b + 1) * BLOCK)
            added = dot(spread[...], halo[c, :, :, block].reshape(2 * HALO, BLOCK))
            if b in (0, BLOCKS - 1):
                added += dot(ghost[c], ends[min(b, 1)])
            register = base[c, :, block] + SCALE * added
            new_register[c, :, block] = register
            new_field[c, :, block] = field[c, :, block] + RK_BETA * register
            for i, (here, there) in enumerate(((new_field, field_out), (new_register, register_out))):
                where = (c, slice(None), pl.ds(b * BLOCK, BLOCK))
                copy = pltpu.make_async_copy(here.at[where], there.at[where], sem.at[i, c, b])
                copy.start()
                copies.append(copy)
    for copy in copies:
        copy.wait()


def body(tiles, test_field, register, velocity, shear_shift):
    field = test_field.reshape(3, CELLS, NX)
    reg = register.reshape(3, CELLS, NX)
    zy = small(np.concatenate([rows_z(FIRST), rows_y(FIRST), rows_y(SECOND) + rows_z(SECOND)], 1))
    outw = small(np.concatenate([rows_out(FIRST), rows_out(SECOND)], 1))
    xw = small(np.concatenate([band(SECOND), -band(FIRST)], 0))
    edgew = small(np.concatenate([band_edges(SECOND), -band_edges(FIRST)], 0))
    stripw = small(np.concatenate([strip_out(SECOND), -strip_out(FIRST)], 0))
    anywhere = pl.BlockSpec(memory_space=pl.ANY)
    vmem = pl.BlockSpec(memory_space=pltpu.VMEM)
    dma = pltpu.SemaphoreType.DMA
    base, kept, halo, strips = pl.pallas_call(
        functools.partial(exchange, tiles),
        out_shape=(
            pltpu.VMEM((3, CELLS, NX), F32),
            pltpu.VMEM((3, CELLS, NX), F32),
            pltpu.VMEM((3, 2, HALO, NX), BF),
            pltpu.VMEM((3, tiles * ROWS, 128), BF),
        ),
        in_specs=[pl.BlockSpec(memory_space=pltpu.SMEM)] + [anywhere] * 8,
        out_specs=(vmem,) * 4,
        scratch_shapes=[
            pltpu.VMEM((3, CELLS, NX), F32),
            pltpu.VMEM((16, 3, ROWS, NX), BF),
            pltpu.VMEM((3, 3 * CELLS, NX), BF),
            pltpu.VMEM((3, 2, HALO, NX), BF),
            pltpu.VMEM(zy.shape, BF),
            pltpu.VMEM(outw.shape, BF),
            pltpu.VMEM(xw.shape, BF),
            pltpu.VMEM(edgew.shape, BF),
            pltpu.VMEM(stripw.shape, BF),
            dma((5,)),
            dma((5,)),
            dma((2, 15)),
            dma((2, 16)),
            dma((2, BLOCKS)),
            dma((2, BLOCKS)),
            dma((tiles,)),
            dma((tiles,)),
        ],
        compiler_params=pltpu.CompilerParams(
            collective_id=0, has_side_effects=True, vmem_limit_bytes=54 * 2**20
        ),
        name="exchange",
    )(jnp.asarray(profiles()), field, reg, velocity, zy, outw, xw, edgew, stripw)

    spread, ends = small(halo_in()), small(strip_in())
    new_field, new_register = pl.pallas_call(
        finish,
        out_shape=(jax.ShapeDtypeStruct((3, CELLS, NX), F32),) * 2,
        in_specs=[pl.BlockSpec(memory_space=pltpu.SMEM)] + [vmem] * 6,
        out_specs=(anywhere, anywhere),
        scratch_shapes=[
            pltpu.VMEM((3, CELLS, 128), BF),
            pltpu.VMEM((3, CELLS, NX), F32),
            pltpu.VMEM((3, CELLS, NX), F32),
            dma((2, 3, BLOCKS)),
        ],
        compiler_params=pltpu.CompilerParams(vmem_limit_bytes=24 * 2**20),
        name="finish",
    )(shear_shift, base, kept, halo, strips, spread, ends)
    return new_field.reshape(test_field.shape), new_register.reshape(register.shape)


def solution(mesh):
    cells = P("tf", None, None, "tile", None)
    return jax.shard_map(
        functools.partial(body, mesh.shape["tile"]),
        mesh=mesh,
        in_specs=(cells, cells, P(None, "tf", "tile", None), P()),
        out_specs=(cells, cells),
        check_vma=False,
    )
```

```python
import functools
import math

import jax
import jax.numpy as jnp
import ml_dtypes
import numpy as np
from jax import lax
from jax.experimental import pallas as pl
from jax.experimental.pallas import tpu as pltpu
from jax.sharding import PartitionSpec as P

BF = jnp.bfloat16
F32 = jnp.float32
TIME_STEP = 0.3
RK_ALPHA = -5.0 / 9.0
RK_BETA = 15.0 / 16.0
SWEEP_SPEED = 0.75
STRETCH_RATE = 0.375
SCALE = TIME_STEP / 60.0

FIRST = {-3: -1, -2: 9, -1: -45, 1: 45, 2: -9, 3: 1}
SECOND = {-3: 2, -2: -27, -1: 270, 0: -490, 1: 270, 2: -27, 3: 2}

NZ, ROWS, NX = 16, 16, 1024
CELLS = NZ * ROWS
BLOCK = 256
BLOCKS = NX // BLOCK
PARTS = ((0, 3), (1,), (2,))
SPANS = ((0, 2), (2, 1), (3, 1))
ORDER = (0, 3, 1, 2)
HALO = 3 * NZ
NEAR = (-2, -1, 1, 2)
FAR = (1, 2, 3)


def band(coefs):
    out = np.zeros((BLOCK, BLOCK))
    for offset, value in coefs.items():
        for x in range(BLOCK):
            if 0 <= x + offset < BLOCK:
                out[x + offset, x] = value
    return out


def band_edges(coefs):
    out = np.zeros((256, BLOCK))
    for offset, value in coefs.items():
        for x in range(BLOCK):
            if x + offset < 0:
                out[128 + x + offset, x] = value
            elif x + offset >= BLOCK:
                out[128 + x + offset - BLOCK, x] = value
    return out


def rows_y(coefs):
    out = np.zeros((CELLS, CELLS))
    for offset, value in coefs.items():
        for y in range(ROWS):
            if 0 <= y + offset < ROWS:
                for z in range(NZ):
                    out[z * ROWS + y, z * ROWS + y + offset] += value
    return out


def rows_z(coefs):
    out = np.zeros((CELLS, CELLS))
    for offset, value in coefs.items():
        for z in range(NZ):
            for y in range(ROWS):
                out[z * ROWS + y, (z + offset) % NZ * ROWS + y] += value
    return out


def rows_out(coefs):
    out = np.zeros((2, 3, NZ, CELLS))
    for z in range(NZ):
        for j in range(3):
            for s in range(3):
                low, high = s - 3 - j, 3 + s - j
                if low in coefs and low >= -3:
                    out[0, j, z, z * ROWS + ROWS - 3 + s] = coefs[low]
                if high <= 3:
                    out[1, j, z, z * ROWS + s] = coefs[high]
    return out.reshape(2 * HALO, CELLS)


def strip_out(coefs):
    out = np.zeros((256, 128))
    for group in range(16):
        for cell in range(3):
            for s in range(3):
                low, high = s - 3 - cell, 3 + s - cell
                if low >= -3:
                    out[253 + s, group * 8 + cell] = coefs[low]
                if high <= 3:
                    out[s, group * 8 + 4 + cell] = coefs[high]
    return out


def halo_in():
    out = np.zeros((CELLS, 2, 3, NZ))
    for z in range(NZ):
        for j in range(3):
            out[z * ROWS + j, 0, j, z] = 1
            out[z * ROWS + ROWS - 3 + j, 1, j, z] = 1
    return out.reshape(CELLS, 2 * HALO)


def strip_in():
    out = np.zeros((2, 128, BLOCK))
    for lane in range(128):
        cell = lane % 4
        if cell < 3:
            if lane % 8 < 4:
                out[0, lane, cell] = 1
            else:
                out[1, lane, BLOCK - 3 + cell] = 1
    return out


def small(array):
    return jnp.asarray(np.asarray(array).astype(ml_dtypes.bfloat16))


def profiles():
    z = np.arange(NZ, dtype=np.float32)
    out = np.zeros((16, 2, NZ), np.float32)
    for k in range(16):
        phase = np.float32(2.0 * math.pi) * np.float32(k // 4 + 1) * z / np.float32(NZ)
        out[k, k % 2] = np.cos(phase) if k // 2 % 2 == 0 else np.sin(phase)
    return out.reshape(-1)


def dot(a, b):
    return jnp.dot(a, b, preferred_element_type=F32)


def exchange(
    tiles, shift, profile, field_hbm, register_hbm, velocity_hbm, zy_hbm, out_hbm, x_hbm, edge_hbm, strip_hbm,
    base, field, halo, wide,
    register, vel, work, sums, zy, outw, xw, edgew, stripw, near,
    load_sem, const_sem, vsend, vrecv, hsend, hrecv, nsend, nrecv, wsend, wrecv, told,
):
    t = lax.axis_index("tile")
    k = lax.axis_index("tf")
    xi, hc = k // 4, k % 4
    core = k % 2
    plus, minus = (xi + 1) % 4, (xi + 3) % 4
    opposite = (xi + 2) % 4
    other = hc + 2 - (hc // 2) * 4
    at_plus, at_minus, at_opposite = plus * 4 + hc, minus * 4 + hc, opposite * 4 + hc
    partner = xi * 4 + other
    sibling = k + 1 - 2 * core

    own_velocity = []
    for i, (low, high, to) in enumerate(((0, 1, 0), (3, 4, 1), (1, 3, 2))):
        source = velocity_hbm.at[:, 0, :, pl.ds(low * BLOCK, (high - low) * BLOCK)]
        target = vel.at[k, :, :, pl.ds(to * BLOCK, (high - low) * BLOCK)]
        own_velocity.append(pltpu.make_async_copy(source, target, load_sem.at[i]))
    load_field = pltpu.make_async_copy(field_hbm, field, load_sem.at[3])
    load_register = pltpu.make_async_copy(register_hbm, register, load_sem.at[4])
    pairs = ((zy_hbm, zy), (out_hbm, outw), (x_hbm, xw), (edge_hbm, edgew), (strip_hbm, stripw))
    consts = [pltpu.make_async_copy(a, b, const_sem.at[i]) for i, (a, b) in enumerate(pairs)]
    for copy in (*own_velocity, load_field, *consts, load_register):
        copy.start()

    barrier = pltpu.get_barrier_semaphore()
    for peer in (at_plus, at_minus, at_opposite, partner, sibling):
        pl.semaphore_signal(barrier, inc=1, device_id={"tf": peer})
    for step in (1, tiles // 2, tiles - 1):
        pl.semaphore_signal(barrier, inc=1, device_id={"tile": (t + step) % tiles})
    pl.semaphore_wait(barrier, 5 + 3)

    def tell(round_, step):
        for side, to in enumerate((step, tiles - step)):
            pl.semaphore_signal(told.at[round_, side], inc=1, device_id={"tile": (t + to) % tiles})

    def hear(round_):
        for side in range(2):
            pl.semaphore_wait(told.at[round_, side], 1)

    tell(0, 1)

    started = []

    def plane_copy(plane, part, kind, peer):
        block = vel.at[plane, :, :, pl.ds(SPANS[part][0] * BLOCK, SPANS[part][1] * BLOCK)]
        return pltpu.make_async_remote_copy(
            src_ref=block,
            dst_ref=block,
            send_sem=vsend.at[part, kind],
            recv_sem=vrecv.at[part, plane],
            device_id={"tf": peer},
        )

    def send(plane, part, kind, peer):
        copy = plane_copy(plane, part, kind, peer)
        copy.start()
        started.append(copy)

    def arrived(plane, part):
        plane_copy(plane, part, 0, sibling).wait_recv()

    def send_own(part):
        for kind, peer in enumerate((partner, at_opposite, at_plus, at_minus, sibling)):
            send(k, part, kind, peer)

    def relay(part):
        arrived(partner, part)
        send(partner, part, 5, at_plus)
        send(partner, part, 6, at_minus)
        send(partner, part, 7, sibling)
        arrived(at_opposite, part)
        send(at_opposite, part, 8, partner)
        send(at_opposite, part, 9, sibling)
        arrived(at_plus, part)
        send(at_plus, part, 10, sibling)
        arrived(at_minus, part)
        send(at_minus, part, 11, sibling)

    def last_relay(part):
        for i, x in enumerate((plus, minus, opposite)):
            arrived(x * 4 + other, part)
            send(x * 4 + other, part, 12 + i, sibling)

    def from_sibling(part):
        for x in range(4):
            for h in range(2):
                arrived(x * 4 + h * 2 + 1 - core, part)

    def emf_of(b):
        block = pl.ds(b * BLOCK, BLOCK)
        stored = pl.ds(ORDER.index(b) * BLOCK, BLOCK)
        xpos = (lax.broadcasted_iota(jnp.int32, (ROWS, BLOCK), 1) + b * BLOCK).astype(F32)
        sweep = -SWEEP_SPEED * (2.0 * xpos / (NX - 1) - 1.0)

        def plane(z, carry):
            rows = pl.ds(pl.multiple_of(z * ROWS, ROWS), ROWS)
            f = [field[c, rows, block] for c in range(3)]
            v = [vel[z, c, :, stored].astype(F32) for c in range(3)]
            summed = [
                (f[0] + profile[k * 32 + z]).astype(BF).astype(F32),
                (f[1] + profile[k * 32 + 16 + z]).astype(BF).astype(F32),
                f[2].astype(BF).astype(F32),
            ]
            emf_x = v[1] * summed[2] - v[2] * summed[1]
            emf_y = v[2] * summed[0] - v[0] * summed[2]
            emf_z = v[0] * summed[1] - v[1] * summed[0]
            mixed = (emf_z - sweep * f[0], -(sweep * f[1]), -emf_x - sweep * f[2])
            for c, value in enumerate((-emf_y, emf_x, emf_z)):
                work[c, rows, block] = value.astype(BF)
            for c in range(3):
                work[c, pl.ds(pl.multiple_of(CELLS + z * ROWS, ROWS), ROWS), block] = mixed[c].astype(BF)
                work[c, pl.ds(pl.multiple_of(2 * CELLS + z * ROWS, ROWS), ROWS), block] = (f[c] * (1.0 / 30.0)).astype(BF)
            return carry

        lax.fori_loop(0, NZ, plane, 0)

    def halo_copies(b):
        block = pl.ds(b * BLOCK, BLOCK)
        out = []
        for side, peer in ((0, (t + 1) % tiles), (1, (t + tiles - 1) % tiles)):
            out.append(
                pltpu.make_async_remote_copy(
                    src_ref=sums.at[:, side, :, block],
                    dst_ref=halo.at[:, side, :, block],
                    send_sem=hsend.at[side, b],
                    recv_sem=hrecv.at[side, b],
                    device_id={"tile": peer},
                )
            )
        return out

    def halo_of(b):
        block = pl.ds(b * BLOCK, BLOCK)
        for c in range(3):
            total = dot(outw[...], work[c, CELLS:, block]).astype(BF)
            for side in range(2):
                sums[c, side, :, block] = total[side * HALO : (side + 1) * HALO]
        for copy in halo_copies(b):
            copy.start()
            started.append(copy)

    def near_copy(i):
        slot = 2 - NEAR[i]
        return pltpu.make_async_remote_copy(
            src_ref=near.at[:, 2],
            dst_ref=near.at[:, slot],
            send_sem=nsend.at[i],
            recv_sem=nrecv.at[slot],
            device_id={"tile": (t + NEAR[i] + tiles) % tiles},
        )

    def wide_copy(i):
        return pltpu.make_async_remote_copy(
            src_ref=wide.at[:, 0],
            dst_ref=wide.at[:, FAR[i]],
            send_sem=wsend.at[i],
            recv_sem=wrecv.at[i],
            device_id={"tile": (t + tiles - 4 * FAR[i]) % tiles},
        )

    def strips_of():
        row = lax.broadcasted_iota(jnp.int32, (CELLS, 128), 0)
        lane = lax.broadcasted_iota(jnp.int32, (CELLS, 128), 1)
        own = (row // ROWS) == (lane // 8)

        def ends(c, part):
            rows = slice(part * CELLS, (part + 1) * CELLS)
            return jnp.concatenate([work[c, rows, :128], work[c, rows, NX - 128 :]], axis=1)

        for c in range(3):
            total = dot(ends(c, 2), stripw[:256])
            if c == 1:
                total += dot(ends(2, 0), stripw[256:])
            if c == 2:
                total += dot(ends(0, 0), stripw[256:])
            packed = jnp.sum(jnp.where(own, total, 0.0).reshape(NZ, ROWS, 128), axis=0)
            near[c, 2] = packed.astype(BF)
        for i in range(4):
            copy = near_copy(i)
            copy.start()
            started.append(copy)

    def shifted_strips():
        for i in range(4):
            near_copy(i).wait_recv()
        row = lax.broadcasted_iota(jnp.int32, (ROWS, 5 * ROWS), 0)
        source = lax.broadcasted_iota(jnp.int32, (ROWS, 5 * ROWS), 1)
        lane = lax.broadcasted_iota(jnp.int32, (ROWS, 128), 1)
        picks = [
            jnp.where(row + ((shift[side] + 2 * ROWS) & (4 * ROWS - 1)) == source, 1.0, 0.0).astype(BF) for side in range(2)
        ]
        for c in range(3):
            low, high = (dot(pick, near[c].reshape(5 * ROWS, 128)) for pick in picks)
            wide[c, 0] = jnp.where(lane % 8 < 4, low, high).astype(BF)
        hear(1)
        for i in range(3):
            copy = wide_copy(i)
            copy.start()
            started.append(copy)

    for copy in own_velocity:
        copy.wait()
    for part in range(3):
        send_own(part)
    for part in range(3):
        relay(part)
    hear(0)
    tell(1, 2)
    load_field.wait()
    for copy in consts:
        copy.wait()
    for part in range(3):
        last_relay(part)
        from_sibling(part)
        for b in PARTS[part]:
            emf_of(b)
        if part == 0:
            strips_of()
        for b in PARTS[part]:
            halo_of(b)
    shifted_strips()

    load_register.wait()
    for b in range(BLOCKS):
        block = slice(b * BLOCK, (b + 1) * BLOCK)

        def ends(c, part):
            rows = slice(part * CELLS, (part + 1) * CELLS)
            before = work[c, rows, b * BLOCK - 128 : b * BLOCK] if b > 0 else None
            after = work[c, rows, (b + 1) * BLOCK : (b + 1) * BLOCK + 128] if b + 1 < BLOCKS else None
            if before is None:
                return after, slice(128, 256)
            if after is None:
                return before, slice(0, 128)
            return jnp.concatenate([before, after], axis=1), slice(0, 256)

        for c in range(3):
            if c < 2:
                total = dot(zy[...], work[c, :, block])
            else:
                total = dot(zy[:, CELLS:], work[c, CELLS:, block])
            total += dot(work[c, 2 * CELLS :, block], xw[:256])
            far, near = ends(c, 2)
            total += dot(far, edgew[:256][near])
            if c > 0:
                source = 2 if c == 1 else 0
                total += dot(work[source, :CELLS, block], xw[256:])
                far, near = ends(source, 0)
                total += dot(far, edgew[256:][near])
            result = RK_ALPHA * register[c, :, block] + SCALE * total
            if c == 1:
                result -= TIME_STEP * STRETCH_RATE * field[0, :, block]
            base[c, :, block] = result

    for b in range(BLOCKS):
        for copy in halo_copies(b):
            copy.wait_recv()
    for i in range(3):
        wide_copy(i).wait_recv()
    for copy in started:
        copy.wait_send()


def finish(shift, base, field, halo, strips, spread, ends, field_out, register_out, ghost, new_field, new_register, sem):
    lane = lax.broadcasted_iota(jnp.int32, (ROWS, 128), 1)
    steps = [((shift[side] + 2 * ROWS) // (4 * ROWS)) % 4 for side in range(2)]
    for c in range(3):
        both = jnp.where(lane % 8 < 4, strips[c, steps[0]], strips[c, steps[1]]).astype(F32)
        for z in range(NZ):
            ghost[c, z * ROWS : (z + 1) * ROWS] = jnp.where(lane // 8 == z, both, 0.0).astype(BF)

    copies = []
    for c in range(3):
        for b in range(BLOCKS):
            block = slice(b * BLOCK, (b + 1) * BLOCK)
            added = dot(spread[...], halo[c, :, :, block].reshape(2 * HALO, BLOCK))
            if b in (0, BLOCKS - 1):
                added += dot(ghost[c], ends[min(b, 1)])
            register = base[c, :, block] + SCALE * added
            new_register[c, :, block] = register
            new_field[c, :, block] = field[c, :, block] + RK_BETA * register
            for i, (here, there) in enumerate(((new_field, field_out), (new_register, register_out))):
                where = (c, slice(None), pl.ds(b * BLOCK, BLOCK))
                copy = pltpu.make_async_copy(here.at[where], there.at[where], sem.at[i, c, b])
                copy.start()
                copies.append(copy)
    for copy in copies:
        copy.wait()


def body(tiles, test_field, register, velocity, shear_shift):
    field = test_field.reshape(3, CELLS, NX)
    reg = register.reshape(3, CELLS, NX)
    zy = small(np.concatenate([rows_z(FIRST), rows_y(FIRST), rows_y(SECOND) + rows_z(SECOND)], 1))
    outw = small(np.concatenate([rows_out(FIRST), rows_out(SECOND)], 1))
    xw = small(np.concatenate([band(SECOND), -band(FIRST)], 0))
    edgew = small(np.concatenate([band_edges(SECOND), -band_edges(FIRST)], 0))
    stripw = small(np.concatenate([strip_out(SECOND), -strip_out(FIRST)], 0))
    anywhere = pl.BlockSpec(memory_space=pl.ANY)
    vmem = pl.BlockSpec(memory_space=pltpu.VMEM)
    dma = pltpu.SemaphoreType.DMA
    base, kept, halo, wide = pl.pallas_call(
        functools.partial(exchange, tiles),
        out_shape=(
            pltpu.VMEM((3, CELLS, NX), F32),
            pltpu.VMEM((3, CELLS, NX), F32),
            pltpu.VMEM((3, 2, HALO, NX), BF),
            pltpu.VMEM((3, 4, ROWS, 128), BF),
        ),
        in_specs=[pl.BlockSpec(memory_space=pltpu.SMEM)] * 2 + [anywhere] * 8,
        out_specs=(vmem,) * 4,
        scratch_shapes=[
            pltpu.VMEM((3, CELLS, NX), F32),
            pltpu.VMEM((16, 3, ROWS, NX), BF),
            pltpu.VMEM((3, 3 * CELLS, NX), BF),
            pltpu.VMEM((3, 2, HALO, NX), BF),
            pltpu.VMEM(zy.shape, BF),
            pltpu.VMEM(outw.shape, BF),
            pltpu.VMEM(xw.shape, BF),
            pltpu.VMEM(edgew.shape, BF),
            pltpu.VMEM(stripw.shape, BF),
            pltpu.VMEM((3, 5, ROWS, 128), BF),
            dma((5,)),
            dma((5,)),
            dma((3, 15)),
            dma((3, 16)),
            dma((2, BLOCKS)),
            dma((2, BLOCKS)),
            dma((4,)),
            dma((5,)),
            dma((3,)),
            dma((3,)),
            pltpu.SemaphoreType.REGULAR((2, 2)),
        ],
        compiler_params=pltpu.CompilerParams(
            collective_id=0, has_side_effects=True, vmem_limit_bytes=54 * 2**20
        ),
        name="exchange",
    )(shear_shift, jnp.asarray(profiles()), field, reg, velocity, zy, outw, xw, edgew, stripw)

    spread, ends = small(halo_in()), small(strip_in())
    new_field, new_register = pl.pallas_call(
        finish,
        out_shape=(jax.ShapeDtypeStruct((3, CELLS, NX), F32),) * 2,
        in_specs=[pl.BlockSpec(memory_space=pltpu.SMEM)] + [vmem] * 6,
        out_specs=(anywhere, anywhere),
        scratch_shapes=[
            pltpu.VMEM((3, CELLS, 128), BF),
            pltpu.VMEM((3, CELLS, NX), F32),
            pltpu.VMEM((3, CELLS, NX), F32),
            dma((2, 3, BLOCKS)),
        ],
        compiler_params=pltpu.CompilerParams(vmem_limit_bytes=24 * 2**20),
        name="finish",
    )(shear_shift, base, kept, halo, wide, spread, ends)
    return new_field.reshape(test_field.shape), new_register.reshape(register.shape)


def solution(mesh):
    cells = P("tf", None, None, "tile", None)
    return jax.shard_map(
        functools.partial(body, mesh.shape["tile"]),
        mesh=mesh,
        in_specs=(cells, cells, P(None, "tf", "tile", None), P()),
        out_specs=(cells, cells),
        check_vma=False,
    )
```

```python
import functools
import math

import jax
import jax.numpy as jnp
import ml_dtypes
import numpy as np
from jax import lax
from jax.experimental import pallas as pl
from jax.experimental.pallas import tpu as pltpu
from jax.sharding import PartitionSpec as P

BF = jnp.bfloat16
F32 = jnp.float32
TIME_STEP = 0.3
RK_ALPHA = -5.0 / 9.0
RK_BETA = 15.0 / 16.0
SWEEP_SPEED = 0.75
STRETCH_RATE = 0.375
SCALE = TIME_STEP / 60.0

FIRST = {-3: -1, -2: 9, -1: -45, 1: 45, 2: -9, 3: 1}
SECOND = {-3: 2, -2: -27, -1: 270, 0: -490, 1: 270, 2: -27, 3: 2}

NZ, ROWS, NX = 16, 16, 1024
CELLS = NZ * ROWS
BLOCK = 256
BLOCKS = NX // BLOCK
PARTS = ((0, 3), (1,), (2,))
SPANS = ((0, 2), (2, 1), (3, 1))
ORDER = (0, 3, 1, 2)
HALO = 3 * NZ
NEAR = (-2, -1, 1, 2)
FAR = (1, 2, 3)
SENT = (0, 2, 1)


def band(coefs):
    out = np.zeros((BLOCK, BLOCK))
    for offset, value in coefs.items():
        for x in range(BLOCK):
            if 0 <= x + offset < BLOCK:
                out[x + offset, x] = value
    return out


def band_edges(coefs):
    out = np.zeros((256, BLOCK))
    for offset, value in coefs.items():
        for x in range(BLOCK):
            if x + offset < 0:
                out[128 + x + offset, x] = value
            elif x + offset >= BLOCK:
                out[128 + x + offset - BLOCK, x] = value
    return out


def rows_y(coefs):
    out = np.zeros((CELLS, CELLS))
    for offset, value in coefs.items():
        for y in range(ROWS):
            if 0 <= y + offset < ROWS:
                for z in range(NZ):
                    out[z * ROWS + y, z * ROWS + y + offset] += value
    return out


def rows_z(coefs):
    out = np.zeros((CELLS, CELLS))
    for offset, value in coefs.items():
        for z in range(NZ):
            for y in range(ROWS):
                out[z * ROWS + y, (z + offset) % NZ * ROWS + y] += value
    return out


def rows_out(coefs):
    out = np.zeros((2, 3, NZ, CELLS))
    for z in range(NZ):
        for j in range(3):
            for s in range(3):
                low, high = s - 3 - j, 3 + s - j
                if low in coefs and low >= -3:
                    out[0, j, z, z * ROWS + ROWS - 3 + s] = coefs[low]
                if high <= 3:
                    out[1, j, z, z * ROWS + s] = coefs[high]
    return out.reshape(2 * HALO, CELLS)


def strip_out(coefs):
    out = np.zeros((256, 128))
    for group in range(16):
        for cell in range(3):
            for s in range(3):
                low, high = s - 3 - cell, 3 + s - cell
                if low >= -3:
                    out[253 + s, group * 8 + cell] = coefs[low]
                if high <= 3:
                    out[s, group * 8 + 4 + cell] = coefs[high]
    return out


def halo_in():
    out = np.zeros((CELLS, 2, 3, NZ))
    for z in range(NZ):
        for j in range(3):
            out[z * ROWS + j, 0, j, z] = 1
            out[z * ROWS + ROWS - 3 + j, 1, j, z] = 1
    return out.reshape(CELLS, 2 * HALO)


def strip_in():
    out = np.zeros((2, 128, BLOCK))
    for lane in range(128):
        cell = lane % 4
        if cell < 3:
            if lane % 8 < 4:
                out[0, lane, cell] = 1
            else:
                out[1, lane, BLOCK - 3 + cell] = 1
    return out


def small(array):
    return jnp.asarray(np.asarray(array).astype(ml_dtypes.bfloat16))


def profiles():
    z = np.arange(NZ, dtype=np.float32)
    out = np.zeros((16, 2, NZ), np.float32)
    for k in range(16):
        phase = np.float32(2.0 * math.pi) * np.float32(k // 4 + 1) * z / np.float32(NZ)
        out[k, k % 2] = np.cos(phase) if k // 2 % 2 == 0 else np.sin(phase)
    return out.reshape(-1)


def dot(a, b):
    return jnp.dot(a, b, preferred_element_type=F32)


def exchange(
    tiles, shift, profile, field_hbm, register_hbm, velocity_hbm, own_hbm, zy_hbm, out_hbm, x_hbm, edge_hbm, strip_hbm,
    base, field, halo, wide,
    register, vel, work, emf, sums, waiting, kept_strips, ownw, zy, outw, xw, edgew, stripw, near,
    load_sem, const_sem, vsend, vrecv, hsend, hrecv, nsend, nrecv, wsend, wrecv, told,
):
    t = lax.axis_index("tile")
    k = lax.axis_index("tf")
    xi, hc = k // 4, k % 4
    core = k % 2
    plus, minus = (xi + 1) % 4, (xi + 3) % 4
    opposite = (xi + 2) % 4
    other = hc + 2 - (hc // 2) * 4
    at_plus, at_minus, at_opposite = plus * 4 + hc, minus * 4 + hc, opposite * 4 + hc
    partner = xi * 4 + other
    sibling = k + 1 - 2 * core

    own_velocity = []
    for i, (low, high, to) in enumerate(((0, 1, 0), (3, 4, 1), (1, 3, 2))):
        source = velocity_hbm.at[:, 0, :, pl.ds(low * BLOCK, (high - low) * BLOCK)]
        target = vel.at[k, :, :, pl.ds(to * BLOCK, (high - low) * BLOCK)]
        own_velocity.append(pltpu.make_async_copy(source, target, load_sem.at[i]))
    load_field = pltpu.make_async_copy(field_hbm, field, load_sem.at[3])
    load_register = pltpu.make_async_copy(register_hbm, register, load_sem.at[4])
    pairs = ((own_hbm, ownw), (zy_hbm, zy), (out_hbm, outw), (x_hbm, xw), (edge_hbm, edgew), (strip_hbm, stripw))
    consts = [pltpu.make_async_copy(a, b, const_sem.at[i]) for i, (a, b) in enumerate(pairs)]
    for copy in (*own_velocity, load_field, *consts, load_register):
        copy.start()

    barrier = pltpu.get_barrier_semaphore()
    for peer in (at_plus, at_minus, at_opposite, partner, sibling):
        pl.semaphore_signal(barrier, inc=1, device_id={"tf": peer})
    for step in (1, tiles // 2, tiles - 1):
        pl.semaphore_signal(barrier, inc=1, device_id={"tile": (t + step) % tiles})
    pl.semaphore_wait(barrier, 5 + 3)

    def tell(round_, step):
        for side, to in enumerate((step, tiles - step)):
            pl.semaphore_signal(told.at[round_, side], inc=1, device_id={"tile": (t + to) % tiles})

    def hear(round_):
        for side in range(2):
            pl.semaphore_wait(told.at[round_, side], 1)

    tell(0, 1)

    started = []

    def plane_copy(plane, part, kind, peer):
        block = vel.at[plane, :, :, pl.ds(SPANS[part][0] * BLOCK, SPANS[part][1] * BLOCK)]
        return pltpu.make_async_remote_copy(
            src_ref=block,
            dst_ref=block,
            send_sem=vsend.at[part, kind],
            recv_sem=vrecv.at[part, plane],
            device_id={"tf": peer},
        )

    def send(plane, part, kind, peer):
        copy = plane_copy(plane, part, kind, peer)
        copy.start()
        started.append(copy)

    def arrived(plane, part):
        plane_copy(plane, part, 0, sibling).wait_recv()

    def send_own(part):
        for kind, peer in enumerate((partner, at_opposite, at_plus, at_minus, sibling)):
            send(k, part, kind, peer)

    def relay(part):
        arrived(partner, part)
        send(partner, part, 5, at_plus)
        send(partner, part, 6, at_minus)
        send(partner, part, 7, sibling)
        arrived(at_opposite, part)
        send(at_opposite, part, 8, partner)
        send(at_opposite, part, 9, sibling)
        arrived(at_plus, part)
        send(at_plus, part, 10, sibling)
        arrived(at_minus, part)
        send(at_minus, part, 11, sibling)

    def last_relay(part):
        for i, x in enumerate((plus, minus, opposite)):
            arrived(x * 4 + other, part)
            send(x * 4 + other, part, 12 + i, sibling)

    def from_sibling(part):
        for x in range(4):
            for h in range(2):
                arrived(x * 4 + h * 2 + 1 - core, part)

    def prepare(b):
        block = pl.ds(b * BLOCK, BLOCK)
        xpos = (lax.broadcasted_iota(jnp.int32, (ROWS, BLOCK), 1) + b * BLOCK).astype(F32)
        sweep = -SWEEP_SPEED * (2.0 * xpos / (NX - 1) - 1.0)

        def plane(z, carry):
            rows = pl.ds(pl.multiple_of(z * ROWS, ROWS), ROWS)
            below = pl.ds(pl.multiple_of(CELLS + z * ROWS, ROWS), ROWS)
            for c in range(3):
                f = field[c, rows, block]
                work[c, rows, block] = (-(sweep * f)).astype(BF)
                work[c, below, block] = (f * (1.0 / 30.0)).astype(BF)
            return carry

        lax.fori_loop(0, NZ, plane, 0)

    def emf_of(b):
        block = pl.ds(b * BLOCK, BLOCK)
        stored = pl.ds(ORDER.index(b) * BLOCK, BLOCK)

        def plane(z, carry):
            rows = pl.ds(pl.multiple_of(z * ROWS, ROWS), ROWS)
            v = [vel[z, c, :, stored].astype(F32) for c in range(3)]
            summed = [
                (field[0, rows, block] + profile[k * 32 + z]).astype(BF).astype(F32),
                (field[1, rows, block] + profile[k * 32 + 16 + z]).astype(BF).astype(F32),
                field[2, rows, block].astype(BF).astype(F32),
            ]
            emf_x = v[1] * summed[2] - v[2] * summed[1]
            emf_y = v[2] * summed[0] - v[0] * summed[2]
            emf_z = v[0] * summed[1] - v[1] * summed[0]
            for i, value in enumerate((-emf_y, emf_z, -emf_x)):
                emf[pl.ds(pl.multiple_of(i * CELLS + z * ROWS, ROWS), ROWS), block] = value.astype(BF)
            return carry

        lax.fori_loop(0, NZ, plane, 0)

    def sides(array, b):
        before = array[:, b * BLOCK - 128 : b * BLOCK] if b > 0 else None
        after = array[:, (b + 1) * BLOCK : (b + 1) * BLOCK + 128] if b + 1 < BLOCKS else None
        if before is None:
            return after, slice(128, 256)
        if after is None:
            return before, slice(0, 128)
        return jnp.concatenate([before, after], axis=1), slice(0, 256)

    def along_x(array, b, weights):
        far, rows = sides(array, b)
        return dot(array[:, b * BLOCK : (b + 1) * BLOCK], xw[weights]) + dot(far, edgew[weights][rows])

    def field_part(b):
        block = slice(b * BLOCK, (b + 1) * BLOCK)
        for place, c in enumerate(SENT):
            total = dot(outw[...], work[c, :, block])
            if place < 2:
                waiting[place, :, block] = total
            else:
                for side in range(2):
                    sums[2, side, :, block] = total[side * HALO : (side + 1) * HALO].astype(BF)
        for c in range(3):
            total = dot(ownw[...], work[c, :, block]) + along_x(work.at[c, CELLS:], b, slice(0, 256))
            result = RK_ALPHA * register[c, :, block] + SCALE * total
            if c == 1:
                result -= TIME_STEP * STRETCH_RATE * field[0, :, block]
            base[c, :, block] = result

    def emf_part_zy(b):
        block = slice(b * BLOCK, (b + 1) * BLOCK)
        base[0, :, block] += SCALE * dot(zy[...], emf[: 2 * CELLS, block])
        base[1, :, block] -= SCALE * dot(zy[:, :CELLS], emf[2 * CELLS :, block])
        base[2, :, block] += SCALE * dot(zy[:, CELLS:], emf[2 * CELLS :, block])

    def emf_part_x(b):
        block = slice(b * BLOCK, (b + 1) * BLOCK)
        base[1, :, block] += SCALE * along_x(emf.at[CELLS : 2 * CELLS], b, slice(256, 512))
        base[2, :, block] += SCALE * along_x(emf.at[:CELLS], b, slice(256, 512))

    def halo_copy(side, places, block, i):
        return pltpu.make_async_remote_copy(
            src_ref=sums.at[places, side, :, block],
            dst_ref=halo.at[places, side, :, block],
            send_sem=hsend.at[side, i],
            recv_sem=hrecv.at[side, i],
            device_id={"tile": (t + (1, tiles - 1)[side]) % tiles},
        )

    def halo_copies(b):
        return [halo_copy(side, pl.ds(0, 2), pl.ds(b * BLOCK, BLOCK), b) for side in range(2)]

    def y_halo_copies():
        return [halo_copy(side, pl.ds(2, 1), pl.ds(0, NX), BLOCKS) for side in range(2)]

    def halo_of(b):
        block = slice(b * BLOCK, (b + 1) * BLOCK)
        for place, first in enumerate((CELLS, 2 * CELLS)):
            total = waiting[place, :, block] + dot(outw[:, :CELLS], emf[first : first + CELLS, block])
            for side in range(2):
                sums[place, side, :, block] = total[side * HALO : (side + 1) * HALO].astype(BF)
        for copy in halo_copies(b):
            copy.start()
            started.append(copy)

    def near_copy(i):
        slot = 2 - NEAR[i]
        return pltpu.make_async_remote_copy(
            src_ref=near.at[:, 2],
            dst_ref=near.at[:, slot],
            send_sem=nsend.at[i],
            recv_sem=nrecv.at[slot],
            device_id={"tile": (t + NEAR[i] + tiles) % tiles},
        )

    def wide_copy(i):
        return pltpu.make_async_remote_copy(
            src_ref=wide.at[:, 0],
            dst_ref=wide.at[:, FAR[i]],
            send_sem=wsend.at[i],
            recv_sem=wrecv.at[i],
            device_id={"tile": (t + tiles - 4 * FAR[i]) % tiles},
        )

    def strip_sum(array, weights):
        row = lax.broadcasted_iota(jnp.int32, (CELLS, 128), 0)
        lane = lax.broadcasted_iota(jnp.int32, (CELLS, 128), 1)
        ends = jnp.concatenate([array[:, :128], array[:, NX - 128 :]], axis=1)
        own = jnp.where((row // ROWS) == (lane // 8), dot(ends, stripw[weights]), 0.0)
        return jnp.sum(own.reshape(NZ, ROWS, 128), axis=0)

    def field_strips():
        for c in range(3):
            kept_strips[c] = strip_sum(work.at[c, CELLS:], slice(0, 256))

    def strips_of():
        near[0, 2] = kept_strips[0].astype(BF)
        near[1, 2] = (kept_strips[1] + strip_sum(emf.at[CELLS : 2 * CELLS], slice(256, 512))).astype(BF)
        near[2, 2] = (kept_strips[2] + strip_sum(emf.at[:CELLS], slice(256, 512))).astype(BF)
        for i in range(4):
            copy = near_copy(i)
            copy.start()
            started.append(copy)

    def shifted_strips():
        for i in range(4):
            near_copy(i).wait_recv()
        row = lax.broadcasted_iota(jnp.int32, (ROWS, 5 * ROWS), 0)
        source = lax.broadcasted_iota(jnp.int32, (ROWS, 5 * ROWS), 1)
        lane = lax.broadcasted_iota(jnp.int32, (ROWS, 128), 1)
        picks = [
            jnp.where(row + ((shift[side] + 2 * ROWS) & (4 * ROWS - 1)) == source, 1.0, 0.0).astype(BF) for side in range(2)
        ]
        for c in range(3):
            low, high = (dot(pick, near[c].reshape(5 * ROWS, 128)) for pick in picks)
            wide[c, 0] = jnp.where(lane % 8 < 4, low, high).astype(BF)
        hear(1)
        for i in range(3):
            copy = wide_copy(i)
            copy.start()
            started.append(copy)

    for copy in own_velocity:
        copy.wait()
    for part in range(3):
        send_own(part)
    load_field.wait()
    for b in range(BLOCKS):
        prepare(b)
    for copy in consts:
        copy.wait()
    load_register.wait()
    field_part(0)
    field_part(3)
    relay(0)
    field_strips()
    field_part(1)
    relay(1)
    field_part(2)
    for copy in y_halo_copies():
        copy.start()
        started.append(copy)
    relay(2)
    hear(0)
    tell(1, 2)

    def finish_part(part):
        last_relay(part)
        from_sibling(part)
        for b in PARTS[part]:
            emf_of(b)
        if part == 0:
            strips_of()
        for b in PARTS[part]:
            halo_of(b)

    finish_part(0)
    emf_part_zy(0)
    finish_part(1)
    emf_part_zy(3)
    emf_part_x(0)
    shifted_strips()
    finish_part(2)
    emf_part_zy(1)
    emf_part_zy(2)
    for b in (1, 2, 3):
        emf_part_x(b)
    for copy in y_halo_copies():
        copy.wait_recv()
    for b in range(BLOCKS):
        for copy in halo_copies(b):
            copy.wait_recv()
    for i in range(3):
        wide_copy(i).wait_recv()
    for copy in started:
        copy.wait_send()


def finish(shift, base, field, halo, strips, spread, ends, field_out, register_out, ghost, new_field, new_register, sem):
    lane = lax.broadcasted_iota(jnp.int32, (ROWS, 128), 1)
    steps = [((shift[side] + 2 * ROWS) // (4 * ROWS)) % 4 for side in range(2)]
    for c in range(3):
        both = jnp.where(lane % 8 < 4, strips[c, steps[0]], strips[c, steps[1]]).astype(F32)
        for z in range(NZ):
            ghost[c, z * ROWS : (z + 1) * ROWS] = jnp.where(lane // 8 == z, both, 0.0).astype(BF)

    copies = []
    for c in range(3):
        for b in range(BLOCKS):
            block = slice(b * BLOCK, (b + 1) * BLOCK)
            added = dot(spread[...], halo[SENT.index(c), :, :, block].reshape(2 * HALO, BLOCK))
            if b in (0, BLOCKS - 1):
                added += dot(ghost[c], ends[min(b, 1)])
            register = base[c, :, block] + SCALE * added
            new_register[c, :, block] = register
            new_field[c, :, block] = field[c, :, block] + RK_BETA * register
            for i, (here, there) in enumerate(((new_field, field_out), (new_register, register_out))):
                where = (c, slice(None), pl.ds(b * BLOCK, BLOCK))
                copy = pltpu.make_async_copy(here.at[where], there.at[where], sem.at[i, c, b])
                copy.start()
                copies.append(copy)
    for copy in copies:
        copy.wait()


def body(tiles, test_field, register, velocity, shear_shift):
    field = test_field.reshape(3, CELLS, NX)
    reg = register.reshape(3, CELLS, NX)
    ownw = small(np.concatenate([rows_y(FIRST), rows_y(SECOND) + rows_z(SECOND)], 1))
    zy = small(np.concatenate([rows_z(FIRST), rows_y(FIRST)], 1))
    outw = small(np.concatenate([rows_out(FIRST), rows_out(SECOND)], 1))
    xw = small(np.concatenate([band(SECOND), -band(FIRST)], 0))
    edgew = small(np.concatenate([band_edges(SECOND), -band_edges(FIRST)], 0))
    stripw = small(np.concatenate([strip_out(SECOND), -strip_out(FIRST)], 0))
    anywhere = pl.BlockSpec(memory_space=pl.ANY)
    vmem = pl.BlockSpec(memory_space=pltpu.VMEM)
    dma = pltpu.SemaphoreType.DMA
    base, kept, halo, wide = pl.pallas_call(
        functools.partial(exchange, tiles),
        out_shape=(
            pltpu.VMEM((3, CELLS, NX), F32),
            pltpu.VMEM((3, CELLS, NX), F32),
            pltpu.VMEM((3, 2, HALO, NX), BF),
            pltpu.VMEM((3, 4, ROWS, 128), BF),
        ),
        in_specs=[pl.BlockSpec(memory_space=pltpu.SMEM)] * 2 + [anywhere] * 9,
        out_specs=(vmem,) * 4,
        scratch_shapes=[
            pltpu.VMEM((3, CELLS, NX), F32),
            pltpu.VMEM((16, 3, ROWS, NX), BF),
            pltpu.VMEM((3, 2 * CELLS, NX), BF),
            pltpu.VMEM((3 * CELLS, NX), BF),
            pltpu.VMEM((3, 2, HALO, NX), BF),
            pltpu.VMEM((2, 2 * HALO, NX), F32),
            pltpu.VMEM((3, ROWS, 128), F32),
            pltpu.VMEM(ownw.shape, BF),
            pltpu.VMEM(zy.shape, BF),
            pltpu.VMEM(outw.shape, BF),
            pltpu.VMEM(xw.shape, BF),
            pltpu.VMEM(edgew.shape, BF),
            pltpu.VMEM(stripw.shape, BF),
            pltpu.VMEM((3, 5, ROWS, 128), BF),
            dma((5,)),
            dma((6,)),
            dma((3, 15)),
            dma((3, 16)),
            dma((2, BLOCKS + 1)),
            dma((2, BLOCKS + 1)),
            dma((4,)),
            dma((5,)),
            dma((3,)),
            dma((3,)),
            pltpu.SemaphoreType.REGULAR((2, 2)),
        ],
        compiler_params=pltpu.CompilerParams(
            collective_id=0, has_side_effects=True, vmem_limit_bytes=54 * 2**20
        ),
        name="exchange",
    )(shear_shift, jnp.asarray(profiles()), field, reg, velocity, ownw, zy, outw, xw, edgew, stripw)

    spread, ends = small(halo_in()), small(strip_in())
    new_field, new_register = pl.pallas_call(
        finish,
        out_shape=(jax.ShapeDtypeStruct((3, CELLS, NX), F32),) * 2,
        in_specs=[pl.BlockSpec(memory_space=pltpu.SMEM)] + [vmem] * 6,
        out_specs=(anywhere, anywhere),
        scratch_shapes=[
            pltpu.VMEM((3, CELLS, 128), BF),
            pltpu.VMEM((3, CELLS, NX), F32),
            pltpu.VMEM((3, CELLS, NX), F32),
            dma((2, 3, BLOCKS)),
        ],
        compiler_params=pltpu.CompilerParams(vmem_limit_bytes=24 * 2**20),
        name="finish",
    )(shear_shift, base, kept, halo, wide, spread, ends)
    return new_field.reshape(test_field.shape), new_register.reshape(register.shape)


def solution(mesh):
    cells = P("tf", None, None, "tile", None)
    return jax.shard_map(
        functools.partial(body, mesh.shape["tile"]),
        mesh=mesh,
        in_specs=(cells, cells, P(None, "tf", "tile", None), P()),
        out_specs=(cells, cells),
        check_vma=False,
    )
```

```python
import functools
import math

import jax
import jax.numpy as jnp
import ml_dtypes
import numpy as np
from jax import lax
from jax.experimental import pallas as pl
from jax.experimental.pallas import tpu as pltpu
from jax.sharding import PartitionSpec as P

BF = jnp.bfloat16
F32 = jnp.float32
TIME_STEP = 0.3
RK_ALPHA = -5.0 / 9.0
RK_BETA = 15.0 / 16.0
SWEEP_SPEED = 0.75
STRETCH_RATE = 0.375
SCALE = TIME_STEP / 60.0

FIRST = {-3: -1, -2: 9, -1: -45, 1: 45, 2: -9, 3: 1}
SECOND = {-3: 2, -2: -27, -1: 270, 0: -490, 1: 270, 2: -27, 3: 2}

NZ, ROWS, NX = 16, 16, 1024
CELLS = NZ * ROWS
BLOCK = 256
BLOCKS = NX // BLOCK
PARTS = (((0, 128), (896, 128)), ((128, 512),), ((640, 256),))
SPANS = tuple(span for part in PARTS for span in part)
WIDTHS = tuple(sum(width for _, width in part) for part in PARTS)
HALO = 3 * NZ
NEAR = (-2, -1, 1, 2)
FAR = (1, 2, 3)
SENT = (0, 2, 1)


def band(coefs):
    out = np.zeros((BLOCK, BLOCK))
    for offset, value in coefs.items():
        for x in range(BLOCK):
            if 0 <= x + offset < BLOCK:
                out[x + offset, x] = value
    return out


def band_edges(coefs):
    out = np.zeros((256, BLOCK))
    for offset, value in coefs.items():
        for x in range(BLOCK):
            if x + offset < 0:
                out[128 + x + offset, x] = value
            elif x + offset >= BLOCK:
                out[128 + x + offset - BLOCK, x] = value
    return out


def rows_y(coefs):
    out = np.zeros((CELLS, CELLS))
    for offset, value in coefs.items():
        for y in range(ROWS):
            if 0 <= y + offset < ROWS:
                for z in range(NZ):
                    out[z * ROWS + y, z * ROWS + y + offset] += value
    return out


def rows_z(coefs):
    out = np.zeros((CELLS, CELLS))
    for offset, value in coefs.items():
        for z in range(NZ):
            for y in range(ROWS):
                out[z * ROWS + y, (z + offset) % NZ * ROWS + y] += value
    return out


def rows_out(coefs):
    out = np.zeros((2, 3, NZ, CELLS))
    for z in range(NZ):
        for j in range(3):
            for s in range(3):
                low, high = s - 3 - j, 3 + s - j
                if low in coefs and low >= -3:
                    out[0, j, z, z * ROWS + ROWS - 3 + s] = coefs[low]
                if high <= 3:
                    out[1, j, z, z * ROWS + s] = coefs[high]
    return out.reshape(2 * HALO, CELLS)


def strip_out(coefs):
    out = np.zeros((256, 128))
    for group in range(16):
        for cell in range(3):
            for s in range(3):
                low, high = s - 3 - cell, 3 + s - cell
                if low >= -3:
                    out[253 + s, group * 8 + cell] = coefs[low]
                if high <= 3:
                    out[s, group * 8 + 4 + cell] = coefs[high]
    return out


def halo_in():
    out = np.zeros((CELLS, 2, 3, NZ))
    for z in range(NZ):
        for j in range(3):
            out[z * ROWS + j, 0, j, z] = 1
            out[z * ROWS + ROWS - 3 + j, 1, j, z] = 1
    return out.reshape(CELLS, 2 * HALO)


def strip_in():
    out = np.zeros((2, 128, BLOCK))
    for lane in range(128):
        cell = lane % 4
        if cell < 3:
            if lane % 8 < 4:
                out[0, lane, cell] = 1
            else:
                out[1, lane, BLOCK - 3 + cell] = 1
    return out


def small(array):
    return jnp.asarray(np.asarray(array).astype(ml_dtypes.bfloat16))


def profiles():
    z = np.arange(NZ, dtype=np.float32)
    out = np.zeros((16, 2, NZ), np.float32)
    for k in range(16):
        phase = np.float32(2.0 * math.pi) * np.float32(k // 4 + 1) * z / np.float32(NZ)
        out[k, k % 2] = np.cos(phase) if k // 2 % 2 == 0 else np.sin(phase)
    return out.reshape(-1)


def stored_at(i):
    return sum(width for _, width in SPANS[:i])


def dot(a, b):
    return jnp.dot(a, b, preferred_element_type=F32)


def exchange(
    tiles, shift, profile, field_hbm, register_hbm, velocity_hbm, own_hbm, zy_hbm, out_hbm, x_hbm, edge_hbm, strip_hbm,
    base, field, halo, wide,
    register, vel, work, emf, sums, waiting, kept_strips, ownw, zy, outw, xw, edgew, stripw, near,
    load_sem, const_sem, vsend, vrecv, csend, crecv, hsend, hrecv, nsend, nrecv, wsend, wrecv, told,
):
    t = lax.axis_index("tile")
    k = lax.axis_index("tf")
    xi, hc = k // 4, k % 4
    core = k % 2
    plus, minus = (xi + 1) % 4, (xi + 3) % 4
    opposite = (xi + 2) % 4
    other = hc + 2 - (hc // 2) * 4
    at_plus, at_minus, at_opposite = plus * 4 + hc, minus * 4 + hc, opposite * 4 + hc
    partner = xi * 4 + other
    sibling = k + 1 - 2 * core

    own_velocity = []
    for i, (start, width) in enumerate(SPANS):
        source = velocity_hbm.at[:, 0, :, pl.ds(start, width)]
        target = vel.at[xi, hc, :, :, pl.ds(stored_at(i), width)]
        own_velocity.append(pltpu.make_async_copy(source, target, load_sem.at[2 + i]))
    load_field = pltpu.make_async_copy(field_hbm, field, load_sem.at[0])
    load_register = pltpu.make_async_copy(register_hbm, register, load_sem.at[1])
    pairs = ((own_hbm, ownw), (zy_hbm, zy), (out_hbm, outw), (x_hbm, xw), (edge_hbm, edgew), (strip_hbm, stripw))
    consts = [pltpu.make_async_copy(a, b, const_sem.at[i]) for i, (a, b) in enumerate(pairs)]
    for copy in (*own_velocity, load_field, *consts, load_register):
        copy.start()

    barrier = pltpu.get_barrier_semaphore()
    for peer in (at_plus, at_minus, at_opposite, partner, sibling):
        pl.semaphore_signal(barrier, inc=1, device_id={"tf": peer})
    for step in (1, tiles // 2, tiles - 1):
        pl.semaphore_signal(barrier, inc=1, device_id={"tile": (t + step) % tiles})
    pl.semaphore_wait(barrier, 5 + 3)

    def tell(round_, step):
        for side, to in enumerate((step, tiles - step)):
            pl.semaphore_signal(told.at[round_, side], inc=1, device_id={"tile": (t + to) % tiles})

    def hear(round_):
        for side in range(2):
            pl.semaphore_wait(told.at[round_, side], 1)

    tell(0, 1)

    started = []

    def lanes(part):
        return pl.ds(sum(WIDTHS[:part]), WIDTHS[part])

    def plane_copy(x, h, part, kind, peer):
        block = vel.at[x, h, :, :, lanes(part)]
        return pltpu.make_async_remote_copy(
            src_ref=block,
            dst_ref=block,
            send_sem=vsend.at[part, kind],
            recv_sem=vrecv.at[part, x, h],
            device_id={"tf": peer},
        )

    def send(x, h, part, kind, peer):
        copy = plane_copy(x, h, part, kind, peer)
        copy.start()
        started.append(copy)

    def arrived(x, h, part):
        plane_copy(x, h, part, 0, sibling).wait_recv()

    def row_copy(h, part, which):
        block = vel.at[:, h, :, :, lanes(part)]
        return pltpu.make_async_remote_copy(
            src_ref=block,
            dst_ref=block,
            send_sem=csend.at[part, which],
            recv_sem=crecv.at[part, which],
            device_id={"tf": sibling},
        )

    def send_row(h, part, which):
        copy = row_copy(h, part, which)
        copy.start()
        started.append(copy)

    def send_own(part):
        for kind, peer in enumerate((partner, at_opposite, at_plus, at_minus)):
            send(xi, hc, part, kind, peer)

    def relay(part):
        arrived(xi, other, part)
        send(xi, other, part, 4, at_plus)
        send(xi, other, part, 5, at_minus)
        arrived(opposite, hc, part)
        send(opposite, hc, part, 6, partner)
        arrived(plus, hc, part)
        arrived(minus, hc, part)
        send_row(hc, part, 0)

    def last_relay(part):
        for x in (plus, minus, opposite):
            arrived(x, other, part)
        send_row(other, part, 1)

    def from_sibling(part):
        for which, h in enumerate((hc, other)):
            row_copy(h + 1 - 2 * core, part, which).wait_recv()

    def prepare(b):
        block = pl.ds(b * BLOCK, BLOCK)
        xpos = (lax.broadcasted_iota(jnp.int32, (ROWS, BLOCK), 1) + b * BLOCK).astype(F32)
        sweep = -SWEEP_SPEED * (2.0 * xpos / (NX - 1) - 1.0)

        def plane(z, carry):
            rows = pl.ds(pl.multiple_of(z * ROWS, ROWS), ROWS)
            below = pl.ds(pl.multiple_of(CELLS + z * ROWS, ROWS), ROWS)
            for c in range(3):
                f = field[c, rows, block]
                work[c, rows, block] = (-(sweep * f)).astype(BF)
                work[c, below, block] = (f * (1.0 / 30.0)).astype(BF)
            return carry

        lax.fori_loop(0, NZ, plane, 0)

    def emf_of(span):
        block = pl.ds(*span)
        stored = pl.ds(stored_at(SPANS.index(span)), span[1])

        def plane(z, carry):
            rows = pl.ds(pl.multiple_of(z * ROWS, ROWS), ROWS)
            v = [vel[z >> 2, z & 3, c, :, stored].astype(F32) for c in range(3)]
            summed = [
                (field[0, rows, block] + profile[k * 32 + z]).astype(BF).astype(F32),
                (field[1, rows, block] + profile[k * 32 + 16 + z]).astype(BF).astype(F32),
                field[2, rows, block].astype(BF).astype(F32),
            ]
            emf_x = v[1] * summed[2] - v[2] * summed[1]
            emf_y = v[2] * summed[0] - v[0] * summed[2]
            emf_z = v[0] * summed[1] - v[1] * summed[0]
            for i, value in enumerate((-emf_y, emf_z, -emf_x)):
                emf[pl.ds(pl.multiple_of(i * CELLS + z * ROWS, ROWS), ROWS), block] = value.astype(BF)
            return carry

        lax.fori_loop(0, NZ, plane, 0, unroll=2)

    def sides(array, b):
        before = array[:, b * BLOCK - 128 : b * BLOCK] if b > 0 else None
        after = array[:, (b + 1) * BLOCK : (b + 1) * BLOCK + 128] if b + 1 < BLOCKS else None
        if before is None:
            return after, slice(128, 256)
        if after is None:
            return before, slice(0, 128)
        return jnp.concatenate([before, after], axis=1), slice(0, 256)

    def along_x(array, b, weights):
        far, rows = sides(array, b)
        return dot(array[:, b * BLOCK : (b + 1) * BLOCK], xw[weights]) + dot(far, edgew[weights][rows])

    def field_part(b):
        block = slice(b * BLOCK, (b + 1) * BLOCK)
        for place, c in enumerate(SENT):
            total = dot(outw[...], work[c, :, block])
            if place < 2:
                waiting[place, :, block] = total
            else:
                for side in range(2):
                    sums[2, side, :, block] = total[side * HALO : (side + 1) * HALO].astype(BF)
        for c in range(3):
            total = dot(ownw[...], work[c, :, block]) + along_x(work.at[c, CELLS:], b, slice(0, 256))
            result = RK_ALPHA * register[c, :, block] + SCALE * total
            if c == 1:
                result -= TIME_STEP * STRETCH_RATE * field[0, :, block]
            base[c, :, block] = result

    def emf_part_zy(span):
        block = pl.ds(*span)
        base[0, :, block] += SCALE * dot(zy[...], emf[: 2 * CELLS, block])
        base[1, :, block] -= SCALE * dot(zy[:, :CELLS], emf[2 * CELLS :, block])
        base[2, :, block] += SCALE * dot(zy[:, CELLS:], emf[2 * CELLS :, block])

    def emf_part_x(b):
        block = slice(b * BLOCK, (b + 1) * BLOCK)
        base[1, :, block] += SCALE * along_x(emf.at[CELLS : 2 * CELLS], b, slice(256, 512))
        base[2, :, block] += SCALE * along_x(emf.at[:CELLS], b, slice(256, 512))

    def halo_copy(side, places, block, i):
        return pltpu.make_async_remote_copy(
            src_ref=sums.at[places, side, :, block],
            dst_ref=halo.at[places, side, :, block],
            send_sem=hsend.at[side, i],
            recv_sem=hrecv.at[side, i],
            device_id={"tile": (t + (1, tiles - 1)[side]) % tiles},
        )

    def halo_copies(span):
        return [halo_copy(side, pl.ds(0, 2), pl.ds(*span), SPANS.index(span)) for side in range(2)]

    def y_halo_copies():
        return [halo_copy(side, pl.ds(2, 1), pl.ds(0, NX), len(SPANS)) for side in range(2)]

    def halo_of(span):
        block = pl.ds(*span)
        for place, first in enumerate((CELLS, 2 * CELLS)):
            total = waiting[place, :, block] + dot(outw[:, :CELLS], emf[first : first + CELLS, block])
            for side in range(2):
                sums[place, side, :, block] = total[side * HALO : (side + 1) * HALO].astype(BF)
        for copy in halo_copies(span):
            copy.start()
            started.append(copy)

    def near_copy(i):
        slot = 2 - NEAR[i]
        return pltpu.make_async_remote_copy(
            src_ref=near.at[:, 2],
            dst_ref=near.at[:, slot],
            send_sem=nsend.at[i],
            recv_sem=nrecv.at[slot],
            device_id={"tile": (t + NEAR[i] + tiles) % tiles},
        )

    def wide_copy(i):
        return pltpu.make_async_remote_copy(
            src_ref=wide.at[:, 0],
            dst_ref=wide.at[:, FAR[i]],
            send_sem=wsend.at[i],
            recv_sem=wrecv.at[i],
            device_id={"tile": (t + tiles - 4 * FAR[i]) % tiles},
        )

    def strip_sum(array, weights):
        row = lax.broadcasted_iota(jnp.int32, (CELLS, 128), 0)
        lane = lax.broadcasted_iota(jnp.int32, (CELLS, 128), 1)
        ends = jnp.concatenate([array[:, :128], array[:, NX - 128 :]], axis=1)
        own = jnp.where((row // ROWS) == (lane // 8), dot(ends, stripw[weights]), 0.0)
        return jnp.sum(own.reshape(NZ, ROWS, 128), axis=0)

    def field_strips():
        for c in range(3):
            kept_strips[c] = strip_sum(work.at[c, CELLS:], slice(0, 256))

    def strips_of():
        near[0, 2] = kept_strips[0].astype(BF)
        near[1, 2] = (kept_strips[1] + strip_sum(emf.at[CELLS : 2 * CELLS], slice(256, 512))).astype(BF)
        near[2, 2] = (kept_strips[2] + strip_sum(emf.at[:CELLS], slice(256, 512))).astype(BF)
        for i in range(4):
            copy = near_copy(i)
            copy.start()
            started.append(copy)

    def shifted_strips():
        for i in range(4):
            near_copy(i).wait_recv()
        row = lax.broadcasted_iota(jnp.int32, (ROWS, 5 * ROWS), 0)
        source = lax.broadcasted_iota(jnp.int32, (ROWS, 5 * ROWS), 1)
        lane = lax.broadcasted_iota(jnp.int32, (ROWS, 128), 1)
        picks = [
            jnp.where(row + ((shift[side] + 2 * ROWS) & (4 * ROWS - 1)) == source, 1.0, 0.0).astype(BF) for side in range(2)
        ]
        for c in range(3):
            low, high = (dot(pick, near[c].reshape(5 * ROWS, 128)) for pick in picks)
            wide[c, 0] = jnp.where(lane % 8 < 4, low, high).astype(BF)
        hear(1)
        for i in range(3):
            copy = wide_copy(i)
            copy.start()
            started.append(copy)

    for copy in own_velocity:
        copy.wait()
    for part in range(len(PARTS)):
        send_own(part)
    load_field.wait()
    for b in range(BLOCKS):
        prepare(b)
    for copy in consts:
        copy.wait()
    load_register.wait()
    field_strips()
    for b in range(BLOCKS):
        field_part(b)
        if b < len(PARTS) - 1:
            relay(b)
    for copy in y_halo_copies():
        copy.start()
        started.append(copy)
    relay(len(PARTS) - 1)
    hear(0)
    tell(1, 2)

    def finish_part(part):
        last_relay(part)
        from_sibling(part)
        for span in PARTS[part]:
            emf_of(span)
        if part == 0:
            strips_of()
        for span in PARTS[part]:
            halo_of(span)

    ready, left = [], list(range(BLOCKS))
    for part in range(len(PARTS)):
        if part == len(PARTS) - 1:
            shifted_strips()
        finish_part(part)
        for span in PARTS[part]:
            emf_part_zy(span)
            ready += range(span[0] // 128, (span[0] + span[1]) // 128)
        for b in list(left):
            tiles_read = range(max(2 * b - 1, 0), min(2 * b + 3, NX // 128))
            if set(tiles_read) <= set(ready):
                emf_part_x(b)
                left.remove(b)
    for copy in y_halo_copies():
        copy.wait_recv()
    for span in SPANS:
        for copy in halo_copies(span):
            copy.wait_recv()
    for i in range(3):
        wide_copy(i).wait_recv()
    for copy in started:
        copy.wait_send()


def finish(shift, base, field, halo, strips, spread, ends, field_out, register_out, ghost, new_field, new_register, sem):
    lane = lax.broadcasted_iota(jnp.int32, (ROWS, 128), 1)
    steps = [((shift[side] + 2 * ROWS) // (4 * ROWS)) % 4 for side in range(2)]
    for c in range(3):
        both = jnp.where(lane % 8 < 4, strips[c, steps[0]], strips[c, steps[1]]).astype(F32)
        for z in range(NZ):
            ghost[c, z * ROWS : (z + 1) * ROWS] = jnp.where(lane // 8 == z, both, 0.0).astype(BF)

    copies = []
    for c in range(3):
        for b in range(BLOCKS):
            block = slice(b * BLOCK, (b + 1) * BLOCK)
            added = dot(spread[...], halo[SENT.index(c), :, :, block].reshape(2 * HALO, BLOCK))
            if b in (0, BLOCKS - 1):
                added += dot(ghost[c], ends[min(b, 1)])
            register = base[c, :, block] + SCALE * added
            new_register[c, :, block] = register
            new_field[c, :, block] = field[c, :, block] + RK_BETA * register
            for i, (here, there) in enumerate(((new_field, field_out), (new_register, register_out))):
                where = (c, slice(None), pl.ds(b * BLOCK, BLOCK))
                copy = pltpu.make_async_copy(here.at[where], there.at[where], sem.at[i, c, b])
                copy.start()
                copies.append(copy)
    for copy in copies:
        copy.wait()


def body(tiles, test_field, register, velocity, shear_shift):
    field = test_field.reshape(3, CELLS, NX)
    reg = register.reshape(3, CELLS, NX)
    ownw = small(np.concatenate([rows_y(FIRST), rows_y(SECOND) + rows_z(SECOND)], 1))
    zy = small(np.concatenate([rows_z(FIRST), rows_y(FIRST)], 1))
    outw = small(np.concatenate([rows_out(FIRST), rows_out(SECOND)], 1))
    xw = small(np.concatenate([band(SECOND), -band(FIRST)], 0))
    edgew = small(np.concatenate([band_edges(SECOND), -band_edges(FIRST)], 0))
    stripw = small(np.concatenate([strip_out(SECOND), -strip_out(FIRST)], 0))
    anywhere = pl.BlockSpec(memory_space=pl.ANY)
    vmem = pl.BlockSpec(memory_space=pltpu.VMEM)
    dma = pltpu.SemaphoreType.DMA
    base, kept, halo, wide = pl.pallas_call(
        functools.partial(exchange, tiles),
        out_shape=(
            pltpu.VMEM((3, CELLS, NX), F32),
            pltpu.VMEM((3, CELLS, NX), F32),
            pltpu.VMEM((3, 2, HALO, NX), BF),
            pltpu.VMEM((3, 4, ROWS, 128), BF),
        ),
        in_specs=[pl.BlockSpec(memory_space=pltpu.SMEM)] * 2 + [anywhere] * 9,
        out_specs=(vmem,) * 4,
        scratch_shapes=[
            pltpu.VMEM((3, CELLS, NX), F32),
            pltpu.VMEM((4, 4, 3, ROWS, NX), BF),
            pltpu.VMEM((3, 2 * CELLS, NX), BF),
            pltpu.VMEM((3 * CELLS, NX), BF),
            pltpu.VMEM((3, 2, HALO, NX), BF),
            pltpu.VMEM((2, 2 * HALO, NX), F32),
            pltpu.VMEM((3, ROWS, 128), F32),
            pltpu.VMEM(ownw.shape, BF),
            pltpu.VMEM(zy.shape, BF),
            pltpu.VMEM(outw.shape, BF),
            pltpu.VMEM(xw.shape, BF),
            pltpu.VMEM(edgew.shape, BF),
            pltpu.VMEM(stripw.shape, BF),
            pltpu.VMEM((3, 5, ROWS, 128), BF),
            dma((2 + len(SPANS),)),
            dma((6,)),
            dma((len(PARTS), 7)),
            dma((len(PARTS), 4, 4)),
            dma((len(PARTS), 2)),
            dma((len(PARTS), 2)),
            dma((2, len(SPANS) + 1)),
            dma((2, len(SPANS) + 1)),
            dma((4,)),
            dma((5,)),
            dma((3,)),
            dma((3,)),
            pltpu.SemaphoreType.REGULAR((2, 2)),
        ],
        compiler_params=pltpu.CompilerParams(
            collective_id=0, has_side_effects=True, vmem_limit_bytes=54 * 2**20
        ),
        name="exchange",
    )(shear_shift, jnp.asarray(profiles()), field, reg, velocity, ownw, zy, outw, xw, edgew, stripw)

    spread, ends = small(halo_in()), small(strip_in())
    new_field, new_register = pl.pallas_call(
        finish,
        out_shape=(jax.ShapeDtypeStruct((3, CELLS, NX), F32),) * 2,
        in_specs=[pl.BlockSpec(memory_space=pltpu.SMEM)] + [vmem] * 6,
        out_specs=(anywhere, anywhere),
        scratch_shapes=[
            pltpu.VMEM((3, CELLS, 128), BF),
            pltpu.VMEM((3, CELLS, NX), F32),
            pltpu.VMEM((3, CELLS, NX), F32),
            dma((2, 3, BLOCKS)),
        ],
        compiler_params=pltpu.CompilerParams(vmem_limit_bytes=24 * 2**20),
        name="finish",
    )(shear_shift, base, kept, halo, wide, spread, ends)
    return new_field.reshape(test_field.shape), new_register.reshape(register.shape)


def solution(mesh):
    cells = P("tf", None, None, "tile", None)
    return jax.shard_map(
        functools.partial(body, mesh.shape["tile"]),
        mesh=mesh,
        in_specs=(cells, cells, P(None, "tf", "tile", None), P()),
        out_specs=(cells, cells),
        check_vma=False,
    )
```
